32 devices in a mesh: seq: 4 (over x, core), exp: 8 (over z, y).
Axes of the slice: x: 2, y: 2, z: 4, core: 2. Of those that a mesh axis runs over, the one named last changes fastest.
Arguments:
- query_heads: bfloat16 [2048, 2048], P('seq', 'exp'), may hold values from -100 to 100
- stretch_pairs: bfloat16 [2, 2, 2048, 128], P(None, None, 'seq'), may hold values from -4.5 to 4.5
- cache_pairs: bfloat16 [2, 2, 16384, 128], P(None, None, 'seq'), may hold values from -4.5 to 4.5
- import_lists: int32 [4, 8], replicated, may hold values from 0 to 31, as said below
- file_lengths: int32 [8], replicated, may hold values from 1 to 1536, 2048 in all
- layer_input: bfloat16 [2048, 2048], P(('seq', 'exp')), may hold values from -60 to 60
- out_weight: bfloat16 [2048, 2048], P('exp'), may hold values from -0.375 to 0.375
- norm_gain: float32 [2048], replicated, may hold values from 0.1 to 1.9
- gate_weight: bfloat16 [32, 2048, 768], P(('seq', 'exp')), may hold values from -0.125 to 0.125
- up_weight: bfloat16 [32, 2048, 768], P(('seq', 'exp')), may hold values from -0.125 to 0.125
- down_weight: bfloat16 [32, 768, 2048], P(('seq', 'exp')), may hold values from -0.21875 to 0.21875
- expert_ids: int32 [2048, 8], P(('seq', 'exp')), may hold values from 0 to 31, all different within a row; in each aligned block of 64 rows (0 to 63, 64 to 127, ...) at most 20 rows name the same one
- route_weights: float32 [2048, 8], P(('seq', 'exp')), may hold values from 0.05 to 0.5
Outputs:
- layer_out: bfloat16 [2048, 2048], P(('seq', 'exp'))
The draws below stay inside these ranges and needn't reach their ends.
Inputs may be any that keep to these rules, and one draw needn't show every extreme that they name: `import_lists`: row i names 8 distinct blocks; block b is held by index b // 8 of seq; a row names at most 2 blocks held by one index, and exactly 2 held by some index. `expert_ids`: in the 64 rows of one device, no expert is named by more than 20 rows. `file_lengths`: the lengths sum to 2048.
All inputs are finite; a program needn't handle non-finite values.
Results may differ from the reference program's by a relative error of at most 0.013.
Values may be sent and summed in bfloat16 or wider, within the bound.
No kernel may reach another device: no remote copies, remote signals or barrier semaphores. Data moves between devices by JAX's collectives and lax.ppermute only.
A program may use at most 128 MiB of HBM per device.

```python
import math
import jax
import jax.numpy as jnp
import numpy as np
from jax import lax

D = 2048
HEADS = 16
KV_HEADS = 2
HD = 128
FFE = 768
TOP = 8
EXPERTS = 32
Q_DEV = 512
STRETCH = 2048
TOK_DEV = 64
CAP_E = 20
BLOCK = 512
BLK_DEV = 8
CACHE_BLOCKS = 32
CACHE_TOK = 16384
IMPORTS = 8
CAP_B = 2
FILES = 8
N_SEQ = 4
N_EXP = 8


def shared_keys(key):
    base = jax.random.fold_in(key, 11)
    return jnp.clip(jax.random.normal(base, (KV_HEADS, STRETCH, HD), jnp.float32), -4.5, 4.5)


def draw_stretch_pairs(key, part):
    keys_used = shared_keys(key)
    values_used = jnp.clip(jax.random.normal(jax.random.fold_in(key, 17), (KV_HEADS, STRETCH, HD), jnp.float32), -4.5, 4.5)
    return jnp.stack([keys_used, values_used]).astype(jnp.bfloat16)


def draw_query_heads(key, part):
    result = 2.5 * jnp.clip(jax.random.normal(jax.random.fold_in(key, 19), (STRETCH, HEADS, HD), jnp.float32), -4.8, 4.8)
    return result.reshape(STRETCH, HEADS * HD).astype(jnp.bfloat16)


def draw_layer_input(key, part):
    low_end = math.log(0.3)
    high_end = math.log(3.0)
    row_scale = jnp.exp(jax.random.uniform(jax.random.fold_in(key, 41), (STRETCH, 1), jnp.float32, low_end, high_end))
    col_scale = jnp.exp(jax.random.uniform(jax.random.fold_in(key, 43), (1, D), jnp.float32, low_end, high_end))
    base = jnp.clip(jax.random.normal(jax.random.fold_in(key, 53), (STRETCH, D), jnp.float32), -6.0, 6.0)
    return (base * row_scale * col_scale).astype(jnp.bfloat16)


def draw_import_lists(key, part):
    list_key = jax.random.fold_in(key, 31)

    def one_row(row_key):
        owner_order = jax.random.permutation(jax.random.fold_in(row_key, 1), N_SEQ)
        slots = jnp.arange(IMPORTS, dtype=jnp.int32)
        remaining = jnp.maximum(slots - CAP_B, 0)
        owners = jnp.where(slots < CAP_B, owner_order[0], owner_order[1 + remaining % (N_SEQ - 1)])
        ranking = jnp.where(slots < CAP_B, slots, remaining // (N_SEQ - 1))
        block_orders = jax.vmap(lambda holder: jax.random.permutation(jax.random.fold_in(jax.random.fold_in(row_key, 2), holder), BLK_DEV))(jnp.arange(N_SEQ, dtype=jnp.int32))
        local_ids = block_orders[owners, ranking]
        return (owners * BLK_DEV + local_ids).astype(jnp.int32)
    row_keys = jax.random.split(list_key, N_SEQ)
    return jax.vmap(one_row)(row_keys).astype(jnp.int32)


def block_scale(rng, extent, cuts, smallest, largest):
    factor_of = 1.0
    for dim, shards_of in cuts:
        heights = jax.random.uniform(jax.random.fold_in(jax.random.fold_in(rng, 6), dim), (shards_of,), jnp.float32, smallest / len(cuts), largest / len(cuts))
        factor_of = factor_of * jnp.repeat(jnp.exp(heights), extent[dim] // shards_of).reshape((-1,) + (1,) * (len(extent) - 1 - dim))
    return factor_of


def split_up(number_of, total, reach, skew):
    weights = [(1 << 20) // math.isqrt(standing ** skew) + 1 for standing in range(2, number_of + 1)]
    surplus, holding = total - reach - (number_of - 1), [1] * (number_of - 1)
    while surplus > 0:
        candidates = [i for i in range(number_of - 1) if holding[i] < reach]
        whole, left = sum([weights[i] for i in candidates]), surplus
        for i in candidates:
            addition = min(reach - holding[i], max(1, left * weights[i] // whole), surplus)
            holding[i] = holding[i] + addition
            surplus = surplus - addition
    return np.array([reach] + holding)


def ragged_sizes(rng, number_of, total, limit, lean):
    if number_of == 2:
        one = jax.random.randint(rng, (), max(1, total - limit), min(limit, total - 1) + 1)
        return jnp.stack([one, total - one])
    tallies = jnp.asarray(split_up(number_of, total, limit, lean), jnp.int32)
    twos = (number_of - 1) // 2
    donor, taker = tallies[1:1 + 2 * twos:2], tallies[2:2 + 2 * twos:2]
    room = jnp.minimum(donor - 1, limit - taker)
    shifted = jax.random.randint(jax.random.fold_in(rng, 1), (twos,), 0, 1 << 20) % (room + 1)
    tallies = tallies.at[1:1 + 2 * twos:2].set(donor - shifted).at[2:2 + 2 * twos:2].set(taker + shifted)
    return tallies[jax.random.permutation(jax.random.fold_in(rng, 2), number_of)]


def deal_out(key, own, number, rows, count, top, most, slope):
    order = jax.random.permutation(key, count)
    packed, usual = load_shares(count, rows * top, most, slope, True), load_shares(count, rows * top, most, slope, False)
    places = jnp.arange(count)

    def named(sizes, turn):
        used = int((sizes > 0).sum())
        fixed = max(1, used // 4)
        shifted = fixed + (places - fixed + turn * (used - fixed)) % max(1, count - fixed)
        return jnp.zeros((count,), jnp.int32).at[order[jnp.where(places < fixed, places, shifted)]].set(jnp.asarray(sizes, jnp.int32))

    sizes = jnp.where(number % 4 == 0, named(packed, number // 4), named(usual, number - number // 4 - 1))
    mixed = jax.random.permutation(jax.random.fold_in(own, 3), count)
    giver, taker = mixed[0:count // 2 * 2:2], mixed[1:count // 2 * 2:2]
    margin = jnp.minimum(sizes[giver] - 1, most - sizes[taker]) // 2
    margin = jnp.where((giver == order[0]) | (taker == order[0]) | (sizes[taker] == 0), 0, jnp.maximum(margin, 0))
    shifted = jax.random.randint(jax.random.fold_in(own, 4), (count // 2,), 0, 1 << 20) % (margin + 1)
    sizes = sizes.at[giver].add(-shifted).at[taker].add(shifted)
    labels = jnp.searchsorted(jnp.cumsum(sizes), jnp.arange(rows * top), side="right").astype(jnp.int32)
    table = labels.reshape(top, rows).T
    table = table[jax.random.permutation(jax.random.fold_in(own, 1), rows)]
    turn = jax.random.randint(jax.random.fold_in(own, 2), (rows, 1), 0, top)
    return jnp.take_along_axis(table, (jnp.arange(top)[None, :] + turn) % top, axis=1)


def load_shares(number_of, total, limit, slope, full):
    portions = [(1 << 20) // math.isqrt(grade ** slope) + 1 for grade in range(1, number_of + 1)]
    largest = limit if full else min(limit, max(-(-total // number_of), total * portions[0] // sum(portions)))
    least = 1 if total - largest >= number_of - 1 else 0
    given, rest = [largest] + [least] * (number_of - 1), total - largest - least * (number_of - 1)
    while rest > 0:
        candidates = [i for i in range(1, number_of) if given[i] < largest] or [i for i in range(1, number_of) if given[i] < limit]
        whole, left = sum([portions[i] for i in candidates]), rest
        for i in candidates:
            extra = min(limit - given[i], max(1, left * portions[i] // whole), rest)
            given[i] = given[i] + extra
            rest = rest - extra
    return np.array(given)


def gaussian(own_key, dims, scale, limit, cuts=(), held_as=jnp.bfloat16):
    loudness = block_scale(own_key, dims, cuts, -0.22, 0.18) if cuts else 1.0
    values = jax.random.normal(own_key, dims, jnp.float32) * scale * loudness
    return jnp.minimum(jnp.maximum(values, -limit), limit).astype(held_as)


def setup_inputs(seed: int = 0) -> dict:
    seeds = jax.random.split(jax.random.key(seed), 14)
    query_heads = draw_query_heads(jax.random.fold_in(seeds[13], 71), 0)
    stretch_pairs = draw_stretch_pairs(jax.random.fold_in(seeds[13], 71), 0)
    cache_pairs = gaussian(seeds[2], (2, KV_HEADS, CACHE_TOK, HD), 1.0, 4.5, ((2, 4),))
    import_lists = draw_import_lists(jax.random.fold_in(seeds[13], 71), 0)
    file_lengths = ragged_sizes(seeds[4], FILES, STRETCH, STRETCH * 3 // 4, 2).astype(jnp.int32)
    layer_input = draw_layer_input(jax.random.fold_in(seeds[13], 71), 0)
    out_weight = gaussian(seeds[6], (HEADS * HD, D), (HEADS * HD // 8) ** -0.5, 0.375, ((0, 8),))
    norm_gain = jnp.clip(1.0 + 0.18 * jax.random.normal(seeds[7], (D,), jnp.float32), 0.1, 1.9)
    gate_weight = gaussian(seeds[8], (EXPERTS, D, FFE), D ** -0.5, 0.125, ((0, 32),))
    up_weight = gaussian(seeds[9], (EXPERTS, D, FFE), D ** -0.5, 0.125, ((0, 32),))
    down_weight = gaussian(seeds[10], (EXPERTS, FFE, D), FFE ** -0.5, 0.21875, ((0, 32),))
    expert_ids_keys = jax.random.split(jax.random.fold_in(seeds[11], 1), STRETCH // TOK_DEV)
    expert_ids_turns = jax.random.permutation(jax.random.fold_in(seeds[11], 3), STRETCH // TOK_DEV)
    expert_ids = jax.vmap(lambda own, number: deal_out(jax.random.fold_in(seeds[11], 2), own, number, TOK_DEV, EXPERTS, TOP, CAP_E, 2))(expert_ids_keys, expert_ids_turns).reshape((STRETCH, TOP))
    route_weights = jnp.clip(jnp.exp(math.log(0.5) - 2.3025851 * jax.random.uniform(seeds[12], (STRETCH, TOP), jnp.float32) ** block_scale(seeds[12], (STRETCH, TOP), ((0, 32),), -0.2, 0.2)), 0.05, 0.5)
    return dict(query_heads=query_heads, stretch_pairs=stretch_pairs, cache_pairs=cache_pairs, import_lists=import_lists, file_lengths=file_lengths, layer_input=layer_input, out_weight=out_weight, norm_gain=norm_gain, gate_weight=gate_weight, up_weight=up_weight, down_weight=down_weight, expert_ids=expert_ids, route_weights=route_weights)


def reference(query_heads, stretch_pairs, cache_pairs, import_lists, file_lengths, layer_input, out_weight, norm_gain, gate_weight, up_weight, down_weight, expert_ids, route_weights):
    score_scale = 1.0 / math.sqrt(HD)
    group_size = HEADS // KV_HEADS
    offsets = (jnp.cumsum(file_lengths) - file_lengths).astype(jnp.int32)
    positions = jnp.arange(STRETCH, dtype=jnp.int32)
    starts = lax.optimization_barrier(jnp.max(jnp.where(offsets[None, :] <= positions[:, None], offsets[None, :], 0), axis=1)).astype(jnp.int32)
    cache_blocks = cache_pairs.reshape(2, KV_HEADS, CACHE_BLOCKS, BLOCK, HD)
    block_rows = 512 if Q_DEV % 512 == 0 else Q_DEV
    block_total = STRETCH // block_rows

    def one_block(number):
        first_row = (number * block_rows).astype(jnp.int32)
        shard = first_row // Q_DEV
        query_pos = first_row + jnp.arange(block_rows, dtype=jnp.int32)
        query_start = lax.dynamic_slice_in_dim(starts, first_row, block_rows)
        listed = import_lists[shard]
        imported = cache_blocks[:, :, listed].reshape(2, KV_HEADS, IMPORTS * BLOCK, HD)
        local_ok = (positions[None, :] <= query_pos[:, None]) & (positions[None, :] >= query_start[:, None])
        query_block = lax.dynamic_slice_in_dim(query_heads, first_row, block_rows, 0)

        def one_head(head):
            kv_head = head // group_size
            query_part = lax.dynamic_slice_in_dim(query_block, (head * HD).astype(jnp.int32), HD, 1)
            local_scores = jnp.dot(query_part, stretch_pairs[0, kv_head].T, preferred_element_type=jnp.float32) * score_scale
            local_scores = jnp.where(local_ok, local_scores, -jnp.inf)
            far_scores = jnp.dot(query_part, imported[0, kv_head].T, preferred_element_type=jnp.float32) * score_scale
            peak = jnp.maximum(lax.optimization_barrier(jnp.max(local_scores, axis=1)), lax.optimization_barrier(jnp.max(far_scores, axis=1)))
            local_w = jnp.where(local_ok, jnp.exp(local_scores - peak[:, None]), 0.0)
            far_w = jnp.exp(far_scores - peak[:, None])
            row_total = lax.optimization_barrier(jnp.sum(local_w, axis=1)) + lax.optimization_barrier(jnp.sum(far_w, axis=1))
            numer = jnp.dot(local_w.astype(jnp.bfloat16), stretch_pairs[1, kv_head], preferred_element_type=jnp.float32)
            numer = numer + jnp.dot(far_w.astype(jnp.bfloat16), imported[1, kv_head], preferred_element_type=jnp.float32)
            return (numer / row_total[:, None]).astype(jnp.bfloat16)
        per_head = lax.map(one_head, jnp.arange(HEADS, dtype=jnp.int32))
        return per_head.transpose(1, 0, 2).reshape(block_rows, HEADS * HD)
    attended = lax.map(one_block, jnp.arange(block_total, dtype=jnp.int32)).reshape(STRETCH, HEADS * HD)
    attn_out = jnp.dot(attended, out_weight, preferred_element_type=jnp.float32)
    residual = layer_input.astype(jnp.float32) + attn_out
    normed = (residual * lax.rsqrt(lax.optimization_barrier(jnp.mean(residual * residual, axis=1, keepdims=True)) + 1e-06) * norm_gain).astype(jnp.bfloat16)
    flat_ids = expert_ids.reshape(-1)
    flat_gates = route_weights.reshape(-1)
    order = jnp.argsort(flat_ids, stable=True).astype(jnp.int32)
    counts = lax.optimization_barrier(jnp.sum((flat_ids[:, None] == jnp.arange(EXPERTS, dtype=jnp.int32)[None, :]).astype(jnp.int32), axis=0)).astype(jnp.int32)
    expert_start = (jnp.cumsum(counts) - counts).astype(jnp.int32)
    load_most = N_SEQ * N_EXP * CAP_E
    order_padded = jnp.concatenate([order, jnp.zeros((load_most,), jnp.int32)])

    def add_expert(combined, expert):
        picks = lax.dynamic_slice_in_dim(order_padded, expert_start[expert], load_most)
        valid = jnp.arange(load_most, dtype=jnp.int32) < counts[expert]
        token_rows = picks // TOP
        inputs = normed[token_rows]
        gate_part = jnp.dot(inputs, gate_weight[expert], preferred_element_type=jnp.float32)
        up_part = jnp.dot(inputs, up_weight[expert], preferred_element_type=jnp.float32)
        hidden = (jax.nn.silu(gate_part) * up_part).astype(jnp.bfloat16)
        outputs = jnp.dot(hidden, down_weight[expert], preferred_element_type=jnp.float32).astype(jnp.bfloat16)
        scaled = outputs.astype(jnp.float32) * flat_gates[picks][:, None]
        target = jnp.where(valid, token_rows, STRETCH).astype(jnp.int32)
        return (combined.at[target].add(scaled, mode='drop'), None)
    combined, unused = lax.scan(add_expert, jnp.zeros((STRETCH, D), jnp.float32), jnp.arange(EXPERTS, dtype=jnp.int32))
    return (residual + combined).astype(jnp.bfloat16)
```

```python
import functools
import math

import jax
import jax.numpy as jnp
from jax import lax
from jax.experimental import pallas as pl
from jax.experimental.pallas import tpu as pltpu
from jax.sharding import Mesh
from jax.sharding import PartitionSpec as P

BLOCK = 512
CAP_B = 2
Z_SIZE = 4
RING = (0, 1, 3, 2)
NEG_FLOOR = -1e30
BF = jnp.bfloat16
F32 = jnp.float32
MIB = 1 << 20
STAT_ROWS = 16


def vmem(count):
    return [pl.BlockSpec(memory_space=pltpu.VMEM)] * count


def params(mib):
    return pltpu.CompilerParams(vmem_limit_bytes=mib * MIB)


def exchange(value, axis, size, hop):
    return lax.ppermute(value, axis, [(i, i ^ hop) for i in range(size)])


def ring_hop(value, hops):
    n = len(RING)
    return lax.ppermute(value, "z", [(RING[i], RING[(i + hops) % n]) for i in range(n)])


def attend_kernel(scale, sc_ref, q_ref, starts_ref, kb0, kb1, vb0, vb1, ks, vs, out_ref):
    rows, width = q_ref.shape
    hd = kb0.shape[-1]
    heads = width // hd
    tile = min(256, rows, width)
    tiles = rows // tile
    eye = lax.broadcasted_iota(jnp.int32, (tile, tile), 0) == lax.broadcasted_iota(
        jnp.int32, (tile, tile), 1
    )
    valid0, valid1, local = sc_ref[2] > 0, sc_ref[3] > 0, sc_ref[4] > 0
    q_first, k_first = sc_ref[5], sc_ref[6]
    nt = (((1,), (1,)), ((), ()))

    def run(with_local):
        stat = jnp.zeros((STAT_ROWS, tile), F32)
        stat_row = lax.broadcasted_iota(jnp.int32, (STAT_ROWS, tile), 0)
        for t in range(tiles):
            rs = slice(t * tile, (t + 1) * tile)
            if with_local:
                kpos = k_first + lax.broadcasted_iota(jnp.int32, (tile, ks.shape[-2]), 1)
                qpos = (
                    q_first
                    + t * tile
                    + lax.broadcasted_iota(jnp.int32, (tile, ks.shape[-2]), 0)
                )
                allowed = (kpos <= qpos) & (kpos >= starts_ref[rs, :])
            for h in range(heads):
                hs = slice(h * hd, (h + 1) * hd)
                q = q_ref[rs, hs]

                def scores(k_ref):
                    k = k_ref[...].reshape(k_ref.shape[-2], hd)
                    return lax.dot_general(q, k, nt, preferred_element_type=F32) * scale

                parts = [
                    jnp.where(valid0, scores(kb0), NEG_FLOOR),
                    jnp.where(valid1, scores(kb1), NEG_FLOOR),
                ]
                values = [vb0, vb1]
                if with_local:
                    parts.append(jnp.where(allowed, scores(ks), NEG_FLOOR))
                    values.append(vs)
                peak = functools.reduce(
                    jnp.maximum, [jnp.max(p, axis=1, keepdims=True) for p in parts]
                )
                total = jnp.zeros((tile, 1), F32)
                numer = jnp.zeros((tile, hd), F32)
                for p, v_ref in zip(parts, values):
                    w = jnp.exp2(p - peak)
                    total = total + jnp.sum(w, axis=1, keepdims=True)
                    v = v_ref[...].reshape(v_ref.shape[-2], hd)
                    numer = numer + jnp.dot(w.astype(BF), v, preferred_element_type=F32)
                out_ref[rs, hs] = (numer / total).astype(BF)
                lse = peak + jnp.log2(total)
                row = jnp.sum(jnp.where(eye, lse, 0.0), axis=0, keepdims=True)
                high = row.astype(BF).astype(F32)
                mid = (row - high).astype(BF).astype(F32)
                low = row - high - mid
                at = (t * heads + h) * 3
                for n, piece in enumerate((high, mid, low)):
                    stat = jnp.where(stat_row == at + n, piece, stat)
        out_ref[rows : rows + STAT_ROWS, :] = jnp.concatenate(
            [stat] * (width // tile), axis=1
        ).astype(BF)

    @pl.when(local)
    def _():
        run(True)

    @pl.when(jnp.logical_not(local))
    def _():
        run(False)


def attend(scalars, queries, starts, cache, stretch, scale):
    rows, width = queries.shape
    hd = cache.shape[-1]
    kv_block = (1, 1, 1, BLOCK, hd)

    def cache_spec(which, slot):
        return pl.BlockSpec(kv_block, lambda i, sc: (which, sc[7], sc[slot], 0, 0))

    def stretch_spec(which):
        return pl.BlockSpec(
            (1, 1) + stretch.shape[2:], lambda i, sc: (which, sc[7], 0, 0)
        )

    whole = lambda shape: pl.BlockSpec(shape, lambda i, sc: (0,) * len(shape))
    return pl.pallas_call(
        functools.partial(attend_kernel, scale),
        grid_spec=pltpu.PrefetchScalarGridSpec(
            num_scalar_prefetch=1,
            grid=(1,),
            in_specs=[
                whole(queries.shape),
                whole(starts.shape),
                cache_spec(0, 0),
                cache_spec(0, 1),
                cache_spec(1, 0),
                cache_spec(1, 1),
                stretch_spec(0),
                stretch_spec(1),
            ],
            out_specs=whole((rows + STAT_ROWS, width)),
        ),
        out_shape=jax.ShapeDtypeStruct((rows + STAT_ROWS, width), BF),
        compiler_params=params(32),
        cost_estimate=pl.CostEstimate(
            flops=4 * rows * width * 3 * BLOCK,
            bytes_accessed=2 * MIB,
            transcendentals=rows * width // hd * 3 * BLOCK,
        ),
        name="attend",
    )(scalars, queries, starts, cache, cache, cache, cache, stretch, stretch)


def merge_kernel(hd, n_parts, order_ref, *refs):
    parts, outs = refs[:n_parts], refs[n_parts : n_parts + Z_SIZE]
    whole = refs[-1]
    rows, width = whole.shape
    heads = width // hd
    tile = min(256, rows, width)
    eye = lax.broadcasted_iota(jnp.int32, (tile, tile), 0) == lax.broadcasted_iota(
        jnp.int32, (tile, tile), 1
    )
    stats = [p[rows : rows + STAT_ROWS, :tile].astype(F32) for p in parts]
    for t in range(rows // tile):
        rs = slice(t * tile, (t + 1) * tile)
        for h in range(heads):
            hs = slice(h * hd, (h + 1) * hd)
            at = (t * heads + h) * 3
            lses = []
            for s in stats:
                row = s[at : at + 1] + s[at + 1 : at + 2] + s[at + 2 : at + 3]
                lses.append(jnp.sum(jnp.where(eye, row, 0.0), axis=1, keepdims=True))
            peak = functools.reduce(jnp.maximum, lses)
            shares = [jnp.exp2(v - peak) for v in lses]
            total = functools.reduce(jnp.add, shares)
            mixed = functools.reduce(
                jnp.add, [s * p[rs, hs].astype(F32) for s, p in zip(shares, parts)]
            )
            whole[rs, hs] = (mixed / total).astype(BF)
    blocks = outs[0].shape[0] // (rows // order_ref.shape[0])
    size = rows // order_ref.shape[0]
    for k in range(Z_SIZE):
        for b in range(blocks):
            first = pl.multiple_of(order_ref[k * blocks + b] * size, size)
            outs[k][b * size : (b + 1) * size, :] = whole[pl.ds(first, size), :]


def merge(parts, order, rows, hd):
    width = parts[0].shape[1]
    out = jax.ShapeDtypeStruct((rows // Z_SIZE, width), BF)
    return pl.pallas_call(
        functools.partial(merge_kernel, hd, len(parts)),
        in_specs=[pl.BlockSpec(memory_space=pltpu.SMEM)] + vmem(len(parts)),
        out_specs=tuple(vmem(Z_SIZE)),
        out_shape=(out,) * Z_SIZE,
        scratch_shapes=[pltpu.VMEM((rows, width), BF)],
        compiler_params=params(24),
        name="merge",
    )(order, *parts)


def project_kernel(core_ref, *refs):
    n = Z_SIZE
    atts, own_w = refs[:n], refs[n]
    same = refs[n + 1 : 2 * n]
    other = refs[2 * n : 3 * n - 1]
    outs = refs[3 * n - 1 :]
    half = own_w.shape[0] // 2
    total = jnp.dot(atts[0][...], own_w[...], preferred_element_type=F32)
    is_first = core_ref[0] == 0
    for k in range(1, n):
        a = atts[k][...]
        lo, hi = a[:, :half], a[:, half:]
        mine = jnp.where(is_first, lo, hi)
        theirs = jnp.where(is_first, hi, lo)
        total += jnp.dot(mine, same[k - 1][...], preferred_element_type=F32)
        total += jnp.dot(theirs, other[k - 1][...], preferred_element_type=F32)
    size = outs[0].shape[0]
    for b, out in enumerate(outs):
        out[...] = total[b * size : (b + 1) * size].astype(BF)


def project(core, atts, own_w, same, other, count):
    rows, width = atts[0].shape[0], own_w.shape[1]
    out = jax.ShapeDtypeStruct((rows // count, width), BF)
    operands = list(atts) + [own_w] + list(same) + list(other)
    return pl.pallas_call(
        project_kernel,
        in_specs=[pl.BlockSpec(memory_space=pltpu.SMEM)] + vmem(len(operands)),
        out_specs=tuple(vmem(count)),
        out_shape=(out,) * count,
        compiler_params=params(24),
        name="project",
    )(core, *operands)


def norm_kernel(x_ref, gain_ref, *refs):
    sums, (res_ref, a_ref, b_ref) = refs[:-3], refs[-3:]
    res = x_ref[...].astype(F32)
    res = res + functools.reduce(jnp.add, [s[...].astype(F32) for s in sums])
    res_ref[...] = res
    scale = lax.rsqrt(jnp.mean(res * res, axis=1, keepdims=True) + 1e-06)
    normed = (res * scale * gain_ref[...]).astype(BF)
    half = normed.shape[1] // 2
    a_ref[...] = normed[:, :half]
    b_ref[...] = normed[:, half:]


def norm(x, gain, sums):
    rows, width = x.shape
    half = jax.ShapeDtypeStruct((rows, width // 2), BF)
    return pl.pallas_call(
        norm_kernel,
        in_specs=vmem(2 + len(sums)),
        out_specs=tuple(vmem(3)),
        out_shape=(jax.ShapeDtypeStruct((rows, width), F32), half, half),
        compiler_params=params(24),
        name="norm",
    )(x, gain.reshape(1, width), *sums)


def expert_kernel(dims, tokcol_ref, tokrow_ref, wcol_ref, *refs):
    blocks, xs, ys, n_f = dims
    n_in = blocks * (xs + ys)
    ins = refs[:n_in]
    weights = (refs[n_in : n_in + 3], refs[n_in + 3 : n_in + 6])
    outs = refs[n_in + 6 : 2 * n_in + 6]
    rows_x, acc, prod = refs[2 * n_in + 6 :]
    tok, half = ins[0].shape[1:]
    group = xs * ys * tok
    slots = tokcol_ref.shape[2]
    step = pl.program_id(0)

    def split(arrays, k):
        arrays = arrays[k * (xs + ys) : (k + 1) * (xs + ys)]
        return arrays[:ys], arrays[ys:]

    @pl.when(step == 0)
    def _():
        for k in range(blocks):
            first, second = split(ins, k)
            pos = lax.broadcasted_iota(jnp.int32, (2 * slots, group), 1)
            want = jnp.concatenate([tokcol_ref[k, 0][:, :1], tokcol_ref[k, 1][:, :1]], axis=0)
            pick = jnp.where(pos == want, 1.0, 0.0).astype(BF)
            left = jnp.concatenate([r[i] for r in first for i in range(xs)], axis=0)
            right = jnp.concatenate([second[x][y] for y in range(ys) for x in range(xs)], axis=0)
            for c, tokens in enumerate((left, right)):
                got = jnp.dot(pick, tokens, preferred_element_type=F32).astype(BF)
                for e in range(2):
                    rows_x[e, k * slots : (k + 1) * slots, c * half : (c + 1) * half] = got[
                        e * slots : (e + 1) * slots
                    ]

    for e in range(2):
        gate_ref, up_ref, down_ref = weights[e]

        @pl.when((step >= e * n_f) & (step < (e + 1) * n_f))
        def _():
            x = rows_x[e]
            gate = jnp.dot(x, gate_ref[0], preferred_element_type=F32)
            up = jnp.dot(x, up_ref[0], preferred_element_type=F32)
            hidden = (gate / (1.0 + jnp.exp(-gate)) * up).astype(BF)
            part = jnp.dot(hidden, down_ref[0], preferred_element_type=F32)

            @pl.when(step == e * n_f)
            def _():
                acc[...] = part

            @pl.when((step > e * n_f) & (step < (e + 1) * n_f - 1))
            def _():
                acc[...] += part

            @pl.when(step == (e + 1) * n_f - 1)
            def _():
                total = acc[...] + part if n_f > 1 else part
                for k in range(blocks):
                    prod[k, e * slots : (e + 1) * slots, :] = (
                        total[k * slots : (k + 1) * slots] * wcol_ref[k, e][:, :1]
                    ).astype(BF)

    @pl.when(step == 2 * n_f - 1)
    def _():
        for k in range(blocks):
            first, second = split(outs, k)
            pos = lax.broadcasted_iota(jnp.int32, (group, 2 * slots), 0)
            put = jnp.where(pos == tokrow_ref[k], 1.0, 0.0).astype(BF)
            for c in range(2):
                got = jnp.dot(
                    put, prod[k, :, c * half : (c + 1) * half], preferred_element_type=F32
                ).astype(BF)
                for y in range(ys):
                    for x in range(xs):
                        at = (y * xs + x) * tok
                        piece = got[at : at + tok]
                        if c == 0:
                            first[y][x] = piece
                        else:
                            second[x][y] = piece


def experts(dims, tokcol, tokrow, wcol, arrays, own, other):
    blocks, xs, ys = dims
    ffe = own[0].shape[2]
    width = own[0].shape[1]
    f_tile = 256 if ffe % 256 == 0 else ffe
    n_f = ffe // f_tile
    slots = tokcol.shape[2]
    whole = lambda a: pl.BlockSpec(a.shape, lambda i: (0,) * len(a.shape))

    def weight_specs(e):
        at = lambda i: jnp.clip(i - e * n_f, 0, n_f - 1)
        wide = pl.BlockSpec((1, width, f_tile), lambda i: (0, 0, at(i)))
        tall = pl.BlockSpec((1, f_tile, width), lambda i: (0, at(i), 0))
        return [wide, wide, tall]

    rows = blocks * slots
    return pl.pallas_call(
        functools.partial(expert_kernel, (blocks, xs, ys, n_f)),
        grid=(2 * n_f,),
        in_specs=[whole(tokcol), whole(tokrow), whole(wcol)]
        + [whole(a) for a in arrays]
        + weight_specs(0)
        + weight_specs(1),
        out_specs=tuple(whole(a) for a in arrays),
        out_shape=tuple(jax.ShapeDtypeStruct(a.shape, BF) for a in arrays),
        scratch_shapes=[
            pltpu.VMEM((2, rows, width), BF),
            pltpu.VMEM((rows, width), F32),
            pltpu.VMEM((blocks, 2 * slots, width), BF),
        ],
        compiler_params=params(48),
        cost_estimate=pl.CostEstimate(
            flops=2 * 2 * rows * width * ffe * 3,
            bytes_accessed=2 * 3 * 2 * width * ffe,
            transcendentals=2 * rows * ffe,
        ),
        name="experts",
    )(tokcol, tokrow, wcol, *arrays, *own, *other)


def add_up(*parts):
    return functools.reduce(jnp.add, [p.astype(F32) for p in parts])


def per_device(
    query_heads,
    stretch_pairs,
    cache_pairs,
    import_lists,
    file_lengths,
    layer_input,
    out_weight,
    norm_gain,
    gate_weight,
    up_weight,
    down_weight,
    expert_ids,
    route_weights,
):
    xs, ys = lax.axis_size("x"), lax.axis_size("y")
    seq_count, exp_count = xs * 2, Z_SIZE * ys
    x_at, core, z_at, y_at = (lax.axis_index(a) for a in ("x", "core", "z", "y"))
    seq_index, exp_index = x_at * 2 + core, z_at * ys + y_at
    q_rows, q_width = query_heads.shape
    _, kv_count, _, hd = stretch_pairs.shape
    local_heads = q_width // hd
    group_size = local_heads * exp_count // kv_count
    kv_index = exp_index * local_heads // group_size
    ring_at = jnp.sum(jnp.where(jnp.array(RING) == z_at, jnp.arange(Z_SIZE), 0))

    hops = range(1, seq_count)
    all_queries = [query_heads] + [
        exchange(query_heads, ("x", "core"), seq_count, hop) for hop in hops
    ]

    weights = (gate_weight, up_weight, down_weight)
    other_weights = [exchange(w, "core", 2, 1) for w in weights]
    half_rows = out_weight.shape[0] // 2
    half_w = lax.dynamic_slice_in_dim(out_weight, core * half_rows, half_rows, 0)
    same_w, piece = [], half_w
    for _ in range(1, Z_SIZE):
        piece = ring_hop(piece, 1)
        same_w.append(piece)
    other_w = [exchange(p, "core", 2, 1) for p in same_w]

    block_count = cache_pairs.shape[2] // BLOCK
    cache = cache_pairs.reshape(2, kv_count, block_count, BLOCK, hd)
    offsets = jnp.cumsum(file_lengths) - file_lengths
    score_scale = math.log2(math.e) / math.sqrt(hd)
    k_first = seq_index * q_rows
    results = []
    for hop in range(seq_count):
        shard = seq_index ^ hop
        positions = shard * q_rows + jnp.arange(q_rows, dtype=jnp.int32)
        starts = jnp.max(
            jnp.where(offsets[None, :] <= positions[:, None], offsets[None, :], 0), axis=1
        )
        listed = lax.dynamic_index_in_dim(import_lists, shard, 0, keepdims=False)
        here = listed // block_count == seq_index
        rank = jnp.cumsum(here.astype(jnp.int32)) - 1
        slot = here[None, :] & (rank[None, :] == jnp.arange(CAP_B, dtype=jnp.int32)[:, None])
        ids = jnp.sum(jnp.where(slot, (listed % block_count)[None, :], 0), axis=1)
        present = jnp.any(slot, axis=1).astype(jnp.int32)
        needed = (k_first <= positions[-1]) & (k_first + q_rows - 1 >= starts[0])
        scalars = jnp.concatenate(
            [
                ids.astype(jnp.int32),
                present,
                jnp.stack([needed.astype(jnp.int32), positions[0], k_first, kv_index]),
            ]
        ).astype(jnp.int32)
        result = attend(
            scalars, all_queries[hop], starts[:, None], cache, stretch_pairs, score_scale
        )
        results.append(result if hop == 0 else exchange(result, ("x", "core"), seq_count, hop))

    order = []
    ring = jnp.array(RING, dtype=jnp.int32)
    for k in range(Z_SIZE):
        z_to = jnp.sum(jnp.where(jnp.arange(Z_SIZE) == (ring_at + k) % Z_SIZE, ring, 0))
        order += [z_to * ys + (y_at ^ b) for b in range(ys)]
    pieces = merge(results, jnp.stack(order).astype(jnp.int32), q_rows, hd)
    attended = [pieces[0]] + [ring_hop(pieces[k], k) for k in range(1, Z_SIZE)]
    shares = project(
        core.reshape(1).astype(jnp.int32), attended, out_weight, same_w, other_w, ys
    )
    sums = [shares[0]] + [exchange(shares[b], "y", ys, b) for b in range(1, ys)]
    residual, left, right = norm(layer_input, norm_gain, sums)

    token_count, width = layer_input.shape
    top_k = expert_ids.shape[1]
    expert_total = seq_count * exp_count
    capacity = min(token_count, max(2, token_count * top_k * 5 // (4 * expert_total)))
    names = jnp.arange(expert_total, dtype=jnp.int32)
    named = expert_ids[:, :, None] == names[None, None, :]
    chosen = jnp.any(named, axis=1)
    route = jnp.sum(jnp.where(named, route_weights[:, :, None], 0.0), axis=1)
    rank = jnp.cumsum(chosen.astype(jnp.int32), axis=0) - 1
    fills = chosen[:, :, None] & (
        rank[:, :, None] == jnp.arange(capacity, dtype=jnp.int32)[None, None, :]
    )
    numbers = jnp.arange(token_count, dtype=jnp.int32)
    slot_token = jnp.sum(jnp.where(fills, numbers[:, None, None] + 1, 0), axis=0) - 1
    slot_route = jnp.sum(jnp.where(fills, route[:, :, None], 0.0), axis=0)
    info = jnp.stack([slot_token.astype(F32), slot_route], axis=1)
    info = info.reshape(xs, 2, Z_SIZE, ys, 2 * capacity).transpose(0, 2, 3, 1, 4)
    peers = xs * Z_SIZE * ys
    info = lax.all_to_all(
        info.reshape(peers, 4 * capacity), ("x", "z", "y"), split_axis=0, concat_axis=0, tiled=True
    )
    sources = [
        ((x_at ^ x) * Z_SIZE + (z_at ^ k)) * ys + (y_at ^ y)
        for k in range(Z_SIZE)
        for y in range(ys)
        for x in range(xs)
    ]
    info = jnp.take(info, jnp.stack(sources), axis=0)
    info = info.reshape(Z_SIZE, ys * xs, 2, 2, capacity)
    info = jnp.where(core == 0, info, info[:, :, ::-1])
    in_group = jnp.arange(ys * xs, dtype=jnp.int32)[None, :, None, None] * token_count
    slot_token = info[:, :, :, 0].astype(jnp.int32)
    slot_token = jnp.where(slot_token >= 0, slot_token + in_group, -1)
    slots = ys * xs * capacity
    slot_token = slot_token.transpose(0, 2, 1, 3).reshape(Z_SIZE, 2, slots)
    slot_route = info[:, :, :, 1].transpose(0, 2, 1, 3).reshape(Z_SIZE, 2, slots)
    tokcol = jnp.broadcast_to(slot_token[..., None], (Z_SIZE, 2, slots, 128))
    wcol = jnp.broadcast_to(slot_route[..., None], (Z_SIZE, 2, slots, 128))
    tokrow = slot_token.reshape(Z_SIZE, 1, 2 * slots)

    gathered = []
    for k in range(Z_SIZE):
        a, b = left, right
        if k:
            a, b = exchange(a, "z", Z_SIZE, k), exchange(b, "z", Z_SIZE, k)
        a = jnp.stack([a] + [exchange(a, "x", xs, r) for r in range(1, xs)])
        b = jnp.stack([b] + [exchange(b, "y", ys, r) for r in range(1, ys)])
        gathered += [a] + [exchange(a, "y", ys, r) for r in range(1, ys)]
        gathered += [b] + [exchange(b, "x", xs, r) for r in range(1, xs)]

    partial = experts(
        (Z_SIZE, xs, ys), tokcol, tokrow, wcol, gathered, weights, other_weights
    )

    finals = []
    for k in reversed(range(Z_SIZE)):
        mine = partial[k * (xs + ys) : (k + 1) * (xs + ys)]
        first, second = mine[:ys], mine[ys:]
        a = add_up(first[0], *[exchange(first[r], "y", ys, r) for r in range(1, ys)])
        b = add_up(second[0], *[exchange(second[r], "x", xs, r) for r in range(1, xs)])
        a = add_up(a[0], *[exchange(a[r].astype(BF), "x", xs, r) for r in range(1, xs)])
        b = add_up(b[0], *[exchange(b[r].astype(BF), "y", ys, r) for r in range(1, ys)])
        if k:
            a = exchange(a.astype(BF), "z", Z_SIZE, k)
            b = exchange(b.astype(BF), "z", Z_SIZE, k)
        finals.append((a, b))
    combined = jnp.concatenate(
        [add_up(*[f[0] for f in finals]), add_up(*[f[1] for f in finals])], axis=1
    )
    return (residual + combined).astype(BF)


def solution(mesh):
    seq, exp = mesh.shape["seq"], mesh.shape["exp"]
    fine = Mesh(
        mesh.devices.reshape(seq // 2, 2, Z_SIZE, exp // Z_SIZE), ("x", "core", "z", "y")
    )
    s, e = ("x", "core"), ("z", "y")
    both = s + e
    in_specs = (
        P(s, e),
        P(None, None, s, None),
        P(None, None, s, None),
        P(),
        P(),
        P(both, None),
        P(e, None),
        P(),
        P(both, None, None),
        P(both, None, None),
        P(both, None, None),
        P(both, None),
        P(both, None),
    )
    return jax.shard_map(
        per_device, mesh=fine, in_specs=in_specs, out_specs=P(both, None), check_vma=False
    )
```

```python
import functools
import math

import jax
import jax.numpy as jnp
from jax import lax
from jax.experimental import pallas as pl
from jax.experimental.pallas import tpu as pltpu
from jax.sharding import Mesh
from jax.sharding import PartitionSpec as P

BLOCK = 512
CAP_B = 2
Z_SIZE = 4
RING = (0, 1, 3, 2)
NEG_FLOOR = -1e30
BF = jnp.bfloat16
F32 = jnp.float32
MIB = 1 << 20
STAT_ROWS = 16
ATT = 5
LAG = 3
FREE = pl.CostEstimate(flops=0, bytes_accessed=0, transcendentals=0)


def vmem(count):
    return [pl.BlockSpec(memory_space=pltpu.VMEM)] * count


def params(mib):
    return pltpu.CompilerParams(vmem_limit_bytes=mib * MIB)


def exchange(value, axis, size, hop):
    return lax.ppermute(value, axis, [(i, i ^ hop) for i in range(size)])


def later(value, than):
    return lax.optimization_barrier((value, than))[0]


def ring_hop(value, hops):
    n = len(RING)
    return lax.ppermute(value, "z", [(RING[i], RING[(i + hops) % n]) for i in range(n)])


def listed_block(hop, per_index, slot, at, lists, lens):
    seq_index = at[0] * 2 + at[1]
    shard = seq_index ^ hop
    found, block, present = jnp.int32(0), jnp.int32(0), jnp.int32(0)
    for n in range(lists.shape[1]):
        named = lists[shard, n]
        here = named // per_index == seq_index
        hit = here & (found == slot)
        block = jnp.where(hit, named % per_index, block)
        present = jnp.where(hit, 1, present)
        found = found + here.astype(jnp.int32)
    return block, present


def attend_kernel(scale, hop, per_index, at, lists, lens, q_ref, kb0, kb1, vb0, vb1, ks, vs, out_ref):
    rows, width = q_ref.shape
    hd = kb0.shape[-1]
    heads = width // hd
    tile = min(256, rows, width)
    tiles = rows // tile
    eye = lax.broadcasted_iota(jnp.int32, (tile, tile), 0) == lax.broadcasted_iota(
        jnp.int32, (tile, tile), 1
    )
    valid = [listed_block(hop, per_index, n, at, lists, lens)[1] > 0 for n in range(CAP_B)]
    always = lists.shape[1] == CAP_B * lists.shape[0]
    seq_index = at[0] * 2 + at[1]
    q_first, k_first = (seq_index ^ hop) * rows, seq_index * rows
    nt = (((1,), (1,)), ((), ()))

    def first_of_file(pos):
        offset, start = jnp.int32(0), jnp.zeros_like(pos)
        for n in range(lens.shape[0]):
            start = jnp.where(offset <= pos, offset, start)
            offset = offset + lens[n]
        return start

    needed = (k_first <= q_first + rows - 1) & (
        k_first + ks.shape[-2] - 1 >= first_of_file(q_first)
    )

    def run(with_local):
        stat = jnp.zeros((STAT_ROWS, tile), F32)
        stat_row = lax.broadcasted_iota(jnp.int32, (STAT_ROWS, tile), 0)
        for t in range(tiles):
            rs = slice(t * tile, (t + 1) * tile)
            if with_local:
                kpos = k_first + lax.broadcasted_iota(jnp.int32, (tile, ks.shape[-2]), 1)
                qpos = q_first + t * tile + lax.broadcasted_iota(jnp.int32, (tile, 1), 0)
                allowed = (kpos <= qpos) & (kpos >= first_of_file(qpos))
            for h in range(heads):
                hs = slice(h * hd, (h + 1) * hd)
                q = q_ref[rs, hs]

                def scores(k_ref):
                    k = k_ref[...].reshape(k_ref.shape[-2], hd)
                    return lax.dot_general(q, k, nt, preferred_element_type=F32) * scale

                parts = [scores(kb0), scores(kb1)]
                if not always:
                    parts = [jnp.where(v, p, NEG_FLOOR) for v, p in zip(valid, parts)]
                values = [vb0, vb1]
                if with_local:
                    parts.append(jnp.where(allowed, scores(ks), NEG_FLOOR))
                    values.append(vs)
                peak = functools.reduce(
                    jnp.maximum, [jnp.max(p, axis=1, keepdims=True) for p in parts]
                )
                total = jnp.zeros((tile, 1), F32)
                numer = jnp.zeros((tile, hd), F32)
                for p, v_ref in zip(parts, values):
                    w = jnp.exp2(p - peak)
                    total = total + jnp.sum(w, axis=1, keepdims=True)
                    v = v_ref[...].reshape(v_ref.shape[-2], hd)
                    numer = numer + jnp.dot(w.astype(BF), v, preferred_element_type=F32)
                out_ref[rs, hs] = (numer / total).astype(BF)
                lse = peak + jnp.log2(total)
                row = jnp.sum(jnp.where(eye, lse, 0.0), axis=0, keepdims=True)
                high = row.astype(BF).astype(F32)
                mid = (row - high).astype(BF).astype(F32)
                low = row - high - mid
                first = (t * heads + h) * 3
                for n, piece in enumerate((high, mid, low)):
                    stat = jnp.where(stat_row == first + n, piece, stat)
        out_ref[rows : rows + STAT_ROWS, :] = jnp.concatenate(
            [stat] * (width // tile), axis=1
        ).astype(BF)

    @pl.when(needed)
    def _():
        run(True)

    @pl.when(jnp.logical_not(needed))
    def _():
        run(False)


def attend(hop, at, lists, lens, queries, cache, stretch, scale, kv_of):
    rows, width = queries.shape
    per_index, hd = cache.shape[2], cache.shape[-1]

    def cache_spec(which, slot):
        def index(i, *sc):
            return which, kv_of(sc[0]), listed_block(hop, per_index, slot, *sc)[0], 0, 0

        return pl.BlockSpec((1, 1, 1, BLOCK, hd), index)

    def stretch_spec(which):
        return pl.BlockSpec(
            (1, 1) + stretch.shape[2:], lambda i, *sc: (which, kv_of(sc[0]), 0, 0)
        )

    whole = lambda shape: pl.BlockSpec(shape, lambda i, *sc: (0,) * len(shape))
    return pl.pallas_call(
        functools.partial(attend_kernel, scale, hop, per_index),
        grid_spec=pltpu.PrefetchScalarGridSpec(
            num_scalar_prefetch=3,
            grid=(1,),
            in_specs=[
                whole(queries.shape),
                cache_spec(0, 0),
                cache_spec(0, 1),
                cache_spec(1, 0),
                cache_spec(1, 1),
                stretch_spec(0),
                stretch_spec(1),
            ],
            out_specs=whole((rows + STAT_ROWS, width)),
        ),
        out_shape=jax.ShapeDtypeStruct((rows + STAT_ROWS, width), BF),
        compiler_params=params(56),
        cost_estimate=pl.CostEstimate(
            flops=ATT * 4 * rows * width * 3 * BLOCK,
            bytes_accessed=2 * MIB,
            transcendentals=rows * width // hd * 3 * BLOCK,
        ),
        name="attend",
    )(at, lists, lens, queries, cache, cache, cache, cache, stretch, stretch)


def ring_place(z):
    return jnp.where(z < 2, z, 5 - z)


def merge_kernel(hd, n_parts, ys, at, *refs):
    parts, outs = refs[:n_parts], refs[n_parts : n_parts + Z_SIZE]
    whole = refs[-1]
    rows, width = whole.shape
    heads = width // hd
    tile = min(256, rows, width)
    eye = lax.broadcasted_iota(jnp.int32, (tile, tile), 0) == lax.broadcasted_iota(
        jnp.int32, (tile, tile), 1
    )
    stats = [p[rows : rows + STAT_ROWS, :tile].astype(F32) for p in parts]
    for t in range(rows // tile):
        rs = slice(t * tile, (t + 1) * tile)
        for h in range(heads):
            hs = slice(h * hd, (h + 1) * hd)
            row_at = (t * heads + h) * 3
            lses = []
            for s in stats:
                row = s[row_at : row_at + 1] + s[row_at + 1 : row_at + 2] + s[row_at + 2 : row_at + 3]
                lses.append(jnp.sum(jnp.where(eye, row, 0.0), axis=1, keepdims=True))
            peak = functools.reduce(jnp.maximum, lses)
            shares = [jnp.exp2(v - peak) for v in lses]
            total = functools.reduce(jnp.add, shares)
            mixed = functools.reduce(
                jnp.add, [s * p[rs, hs].astype(F32) for s, p in zip(shares, parts)]
            )
            whole[rs, hs] = (mixed / total).astype(BF)
    size = rows // (Z_SIZE * ys)
    for k in range(Z_SIZE):
        z_to = ring_place((ring_place(at[2]) + k) % Z_SIZE)
        for b in range(ys):
            first = pl.multiple_of((z_to * ys + (at[3] ^ b)) * size, size)
            outs[k][b * size : (b + 1) * size, :] = whole[pl.ds(first, size), :]


def merge(parts, at, rows, hd, ys):
    width = parts[0].shape[1]
    out = jax.ShapeDtypeStruct((rows // Z_SIZE, width), BF)
    return pl.pallas_call(
        functools.partial(merge_kernel, hd, len(parts), ys),
        in_specs=[pl.BlockSpec(memory_space=pltpu.SMEM)]
        + vmem(len(parts)),
        out_specs=tuple(vmem(Z_SIZE)),
        out_shape=(out,) * Z_SIZE,
        scratch_shapes=[pltpu.VMEM((rows, width), BF)],
        compiler_params=params(24),
        cost_estimate=FREE,
        name="merge",
    )(at, *parts)


def project_kernel(at, *refs):
    n = Z_SIZE
    atts, own_w = refs[:n], refs[n]
    same = refs[n + 1 : 2 * n]
    other = refs[2 * n : 3 * n - 1]
    outs = refs[3 * n - 1 :]
    half = own_w.shape[0] // 2
    total = jnp.dot(atts[0][...], own_w[...], preferred_element_type=F32)
    is_first = at[1] == 0
    for k in range(1, n):
        a = atts[k][...]
        lo, hi = a[:, :half], a[:, half:]
        mine = jnp.where(is_first, lo, hi)
        theirs = jnp.where(is_first, hi, lo)
        total += jnp.dot(mine, same[k - 1][...], preferred_element_type=F32)
        total += jnp.dot(theirs, other[k - 1][...], preferred_element_type=F32)
    size = outs[0].shape[0]
    for b, out in enumerate(outs):
        out[...] = total[b * size : (b + 1) * size].astype(BF)


def project(at, atts, own_w, same, other, count):
    rows, width = atts[0].shape[0], own_w.shape[1]
    out = jax.ShapeDtypeStruct((rows // count, width), BF)
    operands = list(atts) + [own_w] + list(same) + list(other)
    return pl.pallas_call(
        project_kernel,
        in_specs=[pl.BlockSpec(memory_space=pltpu.SMEM)]
        + vmem(len(operands)),
        out_specs=tuple(vmem(count)),
        out_shape=(out,) * count,
        compiler_params=params(24),
        cost_estimate=FREE,
        name="project",
    )(at, *operands)


def norm_kernel(x_ref, gain_ref, *refs):
    sums, (res_ref, a_ref, b_ref) = refs[:-3], refs[-3:]
    res = x_ref[...].astype(F32)
    res = res + functools.reduce(jnp.add, [s[...].astype(F32) for s in sums])
    res_ref[...] = res
    scale = lax.rsqrt(jnp.mean(res * res, axis=1, keepdims=True) + 1e-06)
    normed = (res * scale * gain_ref[...]).astype(BF)
    half = normed.shape[1] // 2
    a_ref[...] = normed[:, :half]
    b_ref[...] = normed[:, half:]


def norm(x, gain, sums):
    rows, width = x.shape
    half = jax.ShapeDtypeStruct((rows, width // 2), BF)
    return pl.pallas_call(
        norm_kernel,
        in_specs=vmem(2 + len(sums)),
        out_specs=tuple(vmem(3)),
        out_shape=(jax.ShapeDtypeStruct((rows, width), F32), half, half),
        compiler_params=params(24),
        cost_estimate=FREE,
        name="norm",
    )(x, gain.reshape(1, width), *sums)


def slots_kernel(dims, capacity, at, ids_ref, route_ref, out_ref):
    xs, ys = dims
    tok = ids_ref.shape[1]
    total = out_ref.shape[0]
    row = lax.broadcasted_iota(jnp.int32, (total, 1), 0)
    side, line = row % 2, row // 2
    x, in_plane = line // (Z_SIZE * ys), line % (Z_SIZE * ys)
    name = (x * 2 + (side ^ at[1])) * (Z_SIZE * ys) + in_plane
    chosen = jnp.zeros((total, tok), F32)
    route = jnp.zeros((total, tok), F32)
    for n in range(ids_ref.shape[0]):
        hit = ids_ref[n : n + 1, :] == name
        chosen = jnp.where(hit, 1.0, chosen)
        route = jnp.where(hit, route_ref[n : n + 1, :], route)
    before = lax.broadcasted_iota(jnp.int32, (tok, tok), 0) < lax.broadcasted_iota(
        jnp.int32, (tok, tok), 1
    )
    rank = jnp.dot(
        chosen.astype(BF), jnp.where(before, 1.0, 0.0).astype(BF), preferred_element_type=F32
    )
    rank = jnp.where(chosen > 0, rank, -1.0)
    number = lax.broadcasted_iota(jnp.int32, (total, tok), 1).astype(F32) + 1.0
    lane = lax.broadcasted_iota(jnp.int32, out_ref.shape, 1)
    out = jnp.zeros(out_ref.shape, F32)
    for n in range(capacity):
        hit = rank == float(n)
        who = jnp.sum(jnp.where(hit, number, 0.0), axis=1, keepdims=True) - 1.0
        share = jnp.sum(jnp.where(hit, route, 0.0), axis=1, keepdims=True)
        out = jnp.where(lane == n, who, out)
        out = jnp.where(lane == capacity + n, share, out)
    out_ref[...] = out


def fill_slots(dims, capacity, total, at, ids, route):
    return pl.pallas_call(
        functools.partial(slots_kernel, dims, capacity),
        in_specs=[pl.BlockSpec(memory_space=pltpu.SMEM)] + vmem(2),
        out_specs=vmem(1)[0],
        out_shape=jax.ShapeDtypeStruct((total, 2 * capacity), F32),
        compiler_params=params(24),
        cost_estimate=FREE,
        name="fill_slots",
    )(at, ids.T, route.T)


def expert_kernel(dims, at, info_ref, *refs):
    blocks, xs, ys, n_f = dims
    n_in, n_out = 2 * blocks * xs * ys, blocks * (xs + ys)
    ins, hbm = refs[:n_in], refs[n_in : n_in + 6]
    outs = refs[n_in + 6 : n_in + 6 + n_out]
    rows_x, acc, prod, gate_v, up_v, down_v, sems = refs[n_in + 6 + n_out :]
    tok, half = ins[0].shape
    group = xs * ys * tok
    capacity = info_ref.shape[1] // 4
    slots = xs * ys * capacity
    both = 2 * slots
    slabs, _, f_tile = gate_v.shape

    copies = []
    for n in range(2 * n_f):
        e, f, slab = n // n_f, n % n_f, n % slabs
        fs = pl.ds(f * f_tile, f_tile)
        copies.append(
            (
                pltpu.make_async_copy(hbm[3 * e].at[0, :, fs], gate_v.at[slab], sems.at[slab, 0]),
                pltpu.make_async_copy(hbm[3 * e + 1].at[0, :, fs], up_v.at[slab], sems.at[slab, 1]),
                pltpu.make_async_copy(hbm[3 * e + 2].at[0, fs, :], down_v.at[slab], sems.at[slab, 2]),
            )
        )
    for three in copies[:slabs]:
        for c in three:
            c.start()

    info = info_ref[...].astype(BF)
    peers = info.shape[0]
    which = lax.broadcasted_iota(jnp.int32, (blocks, peers), 0)
    peer = lax.broadcasted_iota(jnp.int32, (blocks, peers), 1)
    row = lax.broadcasted_iota(jnp.int32, (4 * capacity, both), 0)
    col = lax.broadcasted_iota(jnp.int32, (4 * capacity, both), 1)
    side, source, slot = col // slots, col % slots // capacity, col % capacity
    token = jnp.zeros((blocks, both), F32)
    route = jnp.zeros((blocks, both), F32)
    for g in range(xs * ys):
        back = (ring_place(at[2]) - which) % Z_SIZE
        line = ((at[0] ^ (g % xs)) * Z_SIZE + ring_place(back)) * ys + (at[3] ^ (g // xs))
        mine = jnp.dot(
            jnp.where(peer == line, 1.0, 0.0).astype(BF), info, preferred_element_type=F32
        ).astype(BF)
        for n in range(2):
            spread = (source == g) & (row == (side * 2 + n) * capacity + slot)
            spread = jnp.dot(
                mine, jnp.where(spread, 1.0, 0.0).astype(BF), preferred_element_type=F32
            )
            if n == 0:
                here = lax.broadcasted_iota(jnp.int32, (blocks, both), 1) % slots // capacity == g
                token = jnp.where(here & (spread >= 0), spread + float(g * tok), token)
                token = jnp.where(here & (spread < 0), -1.0, token)
            else:
                route = route + spread

    def onehot(k, value):
        pos = lax.broadcasted_iota(jnp.int32, (group, both), 0).astype(F32)
        return jnp.where(pos == token[k : k + 1], value, 0.0).astype(BF)

    for k in range(blocks):
        mine = ins[2 * k * xs * ys : 2 * (k + 1) * xs * ys]
        pick = onehot(k, 1.0).T
        left = jnp.concatenate([r[...] for r in mine[: xs * ys]], axis=0)
        right = jnp.concatenate([r[...] for r in mine[xs * ys :]], axis=0)
        for c, tokens in enumerate((left, right)):
            got = jnp.dot(pick, tokens, preferred_element_type=F32).astype(BF)
            for e in range(2):
                rows_x[e, k * slots : (k + 1) * slots, c * half : (c + 1) * half] = got[
                    e * slots : (e + 1) * slots
                ]

    for e in range(2):
        for f in range(n_f):
            n = e * n_f + f
            slab = n % slabs
            for c in copies[n]:
                c.wait()
            x = rows_x[e]
            gate = jnp.dot(x, gate_v[slab], preferred_element_type=F32)
            up = jnp.dot(x, up_v[slab], preferred_element_type=F32)
            hidden = (gate / (1.0 + jnp.exp(-gate)) * up).astype(BF)
            part = jnp.dot(hidden, down_v[slab], preferred_element_type=F32)
            if n + slabs < 2 * n_f:
                for c in copies[n + slabs]:
                    c.start()
            if f > 0:
                part = acc[...] + part
            if f < n_f - 1:
                acc[...] = part
            else:
                for k in range(blocks):
                    prod[k, e * slots : (e + 1) * slots, :] = part[
                        k * slots : (k + 1) * slots
                    ].astype(BF)

    for k in range(blocks):
        mine = outs[k * (xs + ys) : (k + 1) * (xs + ys)]
        put = onehot(k, route[k : k + 1])
        for c in range(2):
            got = jnp.dot(
                put, prod[k, :, c * half : (c + 1) * half], preferred_element_type=F32
            ).astype(BF)
            for y in range(ys):
                for x in range(xs):
                    row = (y * xs + x) * tok
                    piece = got[row : row + tok]
                    if c == 0:
                        mine[y][x] = piece
                    else:
                        mine[ys + x][y] = piece


def experts(dims, at, info, arrays, own, other):
    blocks, xs, ys = dims
    width, ffe = own[0].shape[1:]
    f_tile = 256 if ffe % 256 == 0 else ffe
    n_f = ffe // f_tile
    slots = xs * ys * info.shape[1] // 4
    rows = blocks * slots
    any_space = [pl.BlockSpec(memory_space=pl.ANY)] * 6
    slabs = min(3, 2 * n_f)
    half = arrays[0].shape[1]
    outs = [jax.ShapeDtypeStruct((xs, arrays[0].shape[0], half), BF)] * ys
    outs += [jax.ShapeDtypeStruct((ys, arrays[0].shape[0], half), BF)] * xs
    outs = outs * blocks
    return pl.pallas_call(
        functools.partial(expert_kernel, (blocks, xs, ys, n_f)),
        in_specs=[pl.BlockSpec(memory_space=pltpu.SMEM)] + vmem(1 + len(arrays)) + any_space,
        out_specs=tuple(vmem(len(outs))),
        out_shape=tuple(outs),
        scratch_shapes=[
            pltpu.VMEM((2, rows, width), BF),
            pltpu.VMEM((rows, width), F32),
            pltpu.VMEM((blocks, 2 * slots, width), BF),
            pltpu.VMEM((slabs, width, f_tile), BF),
            pltpu.VMEM((slabs, width, f_tile), BF),
            pltpu.VMEM((slabs, f_tile, width), BF),
            pltpu.SemaphoreType.DMA((slabs, 3)),
        ],
        compiler_params=params(52),
        cost_estimate=FREE,
        name="experts",
    )(at, info, *arrays, *own, *other)


def add_up(*parts):
    return functools.reduce(jnp.add, [p.astype(F32) for p in parts])


def per_device(
    query_heads,
    stretch_pairs,
    cache_pairs,
    import_lists,
    file_lengths,
    layer_input,
    out_weight,
    norm_gain,
    gate_weight,
    up_weight,
    down_weight,
    expert_ids,
    route_weights,
):
    xs, ys = lax.axis_size("x"), lax.axis_size("y")
    seq_count, exp_count = xs * 2, Z_SIZE * ys
    x_at, core, z_at, y_at = (lax.axis_index(a) for a in ("x", "core", "z", "y"))
    q_rows, q_width = query_heads.shape
    _, kv_count, _, hd = stretch_pairs.shape
    local_heads = q_width // hd
    group_size = local_heads * exp_count // kv_count
    at = jnp.stack([x_at, core, z_at, y_at]).astype(jnp.int32)

    hops = range(1, seq_count)
    all_queries = [query_heads] + [
        exchange(query_heads, ("x", "core"), seq_count, hop) for hop in hops
    ]

    weights = (gate_weight, up_weight, down_weight)
    other_weights = [exchange(gate_weight, "core", 2, 1)]
    half_rows = out_weight.shape[0] // 2
    half_w = lax.dynamic_slice_in_dim(out_weight, core * half_rows, half_rows, 0)
    same_w = [ring_hop(half_w, 1)]

    block_count = cache_pairs.shape[2] // BLOCK
    cache = cache_pairs.reshape(2, kv_count, block_count, BLOCK, hd)
    score_scale = math.log2(math.e) / math.sqrt(hd)
    kv_of = lambda at: (at[2] * ys + at[3]) * local_heads // group_size
    def part(hop, queries):
        return attend(
            hop, at, import_lists, file_lengths, queries, cache, stretch_pairs, score_scale, kv_of
        )

    all_queries[-1] = later(all_queries[-1], other_weights[0])
    results = [part(hop, queries) for hop, queries in enumerate(all_queries)]
    same_w.append(ring_hop(later(same_w[-1], results[-1]), 1))
    results = results[:1] + [
        exchange(results[hop], ("x", "core"), seq_count, hop) for hop in range(1, seq_count)
    ]
    token_count = layer_input.shape[0]
    top_k = expert_ids.shape[1]
    expert_total = seq_count * exp_count
    capacity = min(token_count, max(2, token_count * top_k * 5 // (4 * expert_total)))
    peers = xs * Z_SIZE * ys
    info = fill_slots((xs, ys), capacity, expert_total, at, later(expert_ids, results[0]), route_weights)
    info = lax.all_to_all(
        info.reshape(peers, 4 * capacity), ("x", "z", "y"), split_axis=0, concat_axis=0, tiled=True
    )

    results[0] = later(results[0], same_w[1])
    pieces = merge(results, at, q_rows, hd, ys)
    pieces = later(list(pieces), info)
    other_weights.append(exchange(later(up_weight, pieces[0]), "core", 2, 1))
    same_w.append(ring_hop(same_w[-1], 1))

    attended = [pieces[0]] + [ring_hop(pieces[k], k) for k in range(1, Z_SIZE)]

    attended[0] = later(attended[0], other_weights[1])
    other_w = [exchange(p, "core", 2, 1) for p in same_w[:-1]]
    other_w.append(exchange(later(same_w[-1], attended[1:]), "core", 2, 1))
    shares = project(at, attended, out_weight, same_w, other_w, ys)
    other_weights.append(exchange(later(down_weight, shares[0]), "core", 2, 1))
    sums = [later(shares[0], other_weights[2])]
    sums += [exchange(shares[b], "y", ys, b) for b in range(1, ys)]
    residual, left, right = norm(layer_input, norm_gain, sums)

    gathered = []
    for k in range(Z_SIZE):
        firsts = [left] + [exchange(left, "x", xs, r) for r in range(1, xs)]
        seconds = [right] + [exchange(right, "y", ys, r) for r in range(1, ys)]
        after_left, after_right = left, right
        if k + 1 < Z_SIZE:
            after_left, after_right = ring_hop(left, 1), ring_hop(right, 1)
        gathered += firsts
        gathered += [exchange(f, "y", ys, r) for r in range(1, ys) for f in firsts]
        by_x = [seconds] + [[exchange(f, "x", xs, r) for f in seconds] for r in range(1, xs)]
        gathered += [by_x[x][y] for y in range(ys) for x in range(xs)]
        left, right = after_left, after_right

    partial = experts(
        (Z_SIZE, xs, ys), at, info, gathered, weights, other_weights
    )

    lines = {"x": [], "y": []}

    def send(value, axis, size, hop, lag=LAG):
        line = lines[axis]
        if lag and len(line) >= lag:
            value, _ = lax.optimization_barrier((value, line[-lag]))
        line.append(exchange(value, axis, size, hop))
        return line[-1]

    total = None
    for k in [*range(1, Z_SIZE), 0]:
        mine = partial[k * (xs + ys) : (k + 1) * (xs + ys)]
        halves = []
        for piles, (far, n_far), (near, n_near) in (
            (mine[:ys], ("y", ys), ("x", xs)),
            (mine[ys:], ("x", xs), ("y", ys)),
        ):
            got = [send(piles[r], far, n_far, r) for r in range(1, n_far)]
            halves.append((add_up(piles[0], *got), near, n_near))
        halves = [
            add_up(h[0], *[send(h[r].astype(BF), near, n, r) for r in range(1, n)])
            for h, near, n in halves
        ]
        if total is not None:
            halves = [add_up(h, t) for h, t in zip(halves, ring_hop(total, 1))]
        total = jnp.stack(halves).astype(BF) if k else halves
    return (residual + jnp.concatenate(total, axis=1)).astype(BF)


def solution(mesh):
    seq, exp = mesh.shape["seq"], mesh.shape["exp"]
    fine = Mesh(
        mesh.devices.reshape(seq // 2, 2, Z_SIZE, exp // Z_SIZE), ("x", "core", "z", "y")
    )
    s, e = ("x", "core"), ("z", "y")
    both = s + e
    in_specs = (
        P(s, e),
        P(None, None, s, None),
        P(None, None, s, None),
        P(),
        P(),
        P(both, None),
        P(e, None),
        P(),
        P(both, None, None),
        P(both, None, None),
        P(both, None, None),
        P(both, None),
        P(both, None),
    )
    return jax.shard_map(
        per_device, mesh=fine, in_specs=in_specs, out_specs=P(both, None), check_vma=False
    )
```

```python
import functools
import math

import jax
import jax.numpy as jnp
from jax import lax
from jax.experimental import pallas as pl
from jax.experimental.pallas import tpu as pltpu
from jax.sharding import Mesh
from jax.sharding import PartitionSpec as P

BLOCK = 512
CAP_B = 2
Z_SIZE = 4
RING = (0, 1, 3, 2)
NEG_FLOOR = -1e30
BF = jnp.bfloat16
F32 = jnp.float32
MIB = 1 << 20
STAT_ROWS = 16
TAIL = 128
ATT = 10
LAG = 3
FREE = pl.CostEstimate(flops=0, bytes_accessed=0, transcendentals=0)


def vmem(count):
    return [pl.BlockSpec(memory_space=pltpu.VMEM)] * count


def params(mib):
    return pltpu.CompilerParams(vmem_limit_bytes=mib * MIB)


def exchange(value, axis, size, hop):
    return lax.ppermute(value, axis, [(i, i ^ hop) for i in range(size)])


def later(value, than):
    return lax.optimization_barrier((value, than))[0]


def ring_hop(value, hops):
    n = len(RING)
    return lax.ppermute(value, "z", [(RING[i], RING[(i + hops) % n]) for i in range(n)])


def listed_block(hop, per_index, slot, at, lists, lens):
    seq_index = at[0] * 2 + at[1]
    shard = seq_index ^ hop
    found, block, present = jnp.int32(0), jnp.int32(0), jnp.int32(0)
    for n in range(lists.shape[1]):
        named = lists[shard, n]
        here = named // per_index == seq_index
        hit = here & (found == slot)
        block = jnp.where(hit, named % per_index, block)
        present = jnp.where(hit, 1, present)
        found = found + here.astype(jnp.int32)
    return block, present


def attend_kernel(scale, hop, per_index, at, lists, lens, q_ref, kb0, kb1, vb0, vb1, ks, vs, out_ref):
    rows, width = q_ref.shape
    hd = kb0.shape[-1]
    heads = width // hd
    tile = min(256, rows, width)
    tiles = rows // tile
    eye = lax.broadcasted_iota(jnp.int32, (tile, tile), 0) == lax.broadcasted_iota(
        jnp.int32, (tile, tile), 1
    )
    valid = [listed_block(hop, per_index, n, at, lists, lens)[1] > 0 for n in range(CAP_B)]
    always = lists.shape[1] == CAP_B * lists.shape[0]
    seq_index = at[0] * 2 + at[1]
    q_first, k_first = (seq_index ^ hop) * rows, seq_index * rows
    nt = (((1,), (1,)), ((), ()))

    def first_of_file(pos):
        offset, start = jnp.int32(0), jnp.zeros_like(pos)
        for n in range(lens.shape[0]):
            start = jnp.where(offset <= pos, offset, start)
            offset = offset + lens[n]
        return start

    needed = (k_first <= q_first + rows - 1) & (
        k_first + ks.shape[-2] - 1 >= first_of_file(q_first)
    )

    def run(with_local):
        stat_row = lax.broadcasted_iota(jnp.int32, (STAT_ROWS, tile), 0)

        def step(n, stat):
            t, h = n // heads, n % heads
            rs = pl.ds(pl.multiple_of(t * tile, tile), tile)
            hs = pl.ds(pl.multiple_of(h * hd, hd), hd)
            q = q_ref[rs, hs]

            def scores(k_ref):
                k = k_ref[...].reshape(k_ref.shape[-2], hd)
                return lax.dot_general(q, k, nt, preferred_element_type=F32) * scale

            parts = [scores(kb0), scores(kb1)]
            if not always:
                parts = [jnp.where(v, p, NEG_FLOOR) for v, p in zip(valid, parts)]
            values = [vb0, vb1]
            if with_local:
                kpos = k_first + lax.broadcasted_iota(jnp.int32, (tile, ks.shape[-2]), 1)
                qpos = q_first + t * tile + lax.broadcasted_iota(jnp.int32, (tile, 1), 0)
                allowed = (kpos <= qpos) & (kpos >= first_of_file(qpos))
                parts.append(jnp.where(allowed, scores(ks), NEG_FLOOR))
                values.append(vs)
            peak = functools.reduce(
                jnp.maximum, [jnp.max(p, axis=1, keepdims=True) for p in parts]
            )
            total = jnp.zeros((tile, 1), F32)
            numer = jnp.zeros((tile, hd), F32)
            for p, v_ref in zip(parts, values):
                w = jnp.exp2(p - peak)
                total = total + jnp.sum(w, axis=1, keepdims=True)
                v = v_ref[...].reshape(v_ref.shape[-2], hd)
                numer = numer + jnp.dot(w.astype(BF), v, preferred_element_type=F32)
            out_ref[rs, hs] = (numer / total).astype(BF)
            lse = peak + jnp.log2(total)
            row = jnp.sum(jnp.where(eye, lse, 0.0), axis=0, keepdims=True)
            high = row.astype(BF).astype(F32)
            mid = (row - high).astype(BF).astype(F32)
            low = row - high - mid
            for i, piece in enumerate((high, mid, low)):
                stat = jnp.where(stat_row == 3 * n + i, piece, stat)
            return stat

        stat = lax.fori_loop(0, tiles * heads, step, jnp.zeros((STAT_ROWS, tile), F32))
        out_ref[rows : rows + STAT_ROWS, :] = jnp.concatenate(
            [stat] * (width // tile), axis=1
        ).astype(BF)

    @pl.when(needed)
    def _():
        run(True)

    @pl.when(jnp.logical_not(needed))
    def _():
        run(False)


def attend(hop, at, lists, lens, queries, cache, stretch, scale, kv_of):
    rows, width = queries.shape
    per_index, hd = cache.shape[2], cache.shape[-1]

    def cache_spec(which, slot):
        def index(i, *sc):
            return which, kv_of(sc[0]), listed_block(hop, per_index, slot, *sc)[0], 0, 0

        return pl.BlockSpec((1, 1, 1, BLOCK, hd), index)

    def stretch_spec(which):
        return pl.BlockSpec(
            (1, 1) + stretch.shape[2:], lambda i, *sc: (which, kv_of(sc[0]), 0, 0)
        )

    whole = lambda shape: pl.BlockSpec(shape, lambda i, *sc: (0,) * len(shape))
    return pl.pallas_call(
        functools.partial(attend_kernel, scale, hop, per_index),
        grid_spec=pltpu.PrefetchScalarGridSpec(
            num_scalar_prefetch=3,
            grid=(1,),
            in_specs=[
                whole(queries.shape),
                cache_spec(0, 0),
                cache_spec(0, 1),
                cache_spec(1, 0),
                cache_spec(1, 1),
                stretch_spec(0),
                stretch_spec(1),
            ],
            out_specs=whole((rows + STAT_ROWS, width)),
        ),
        out_shape=jax.ShapeDtypeStruct((rows + STAT_ROWS, width), BF),
        compiler_params=params(56),
        cost_estimate=pl.CostEstimate(
            flops=ATT * 4 * rows * width * 3 * BLOCK,
            bytes_accessed=2 * MIB,
            transcendentals=rows * width // hd * 3 * BLOCK,
        ),
        name="attend",
    )(at, lists, lens, queries, cache, cache, cache, cache, stretch, stretch)


def ring_place(z):
    return jnp.where(z < 2, z, 5 - z)


def merge_kernel(hd, n_parts, ys, at, *refs):
    parts, outs = refs[:n_parts], refs[n_parts : n_parts + Z_SIZE]
    whole = refs[-1]
    rows, width = whole.shape
    heads = width // hd
    tile = min(256, rows, width)
    eye = lax.broadcasted_iota(jnp.int32, (tile, tile), 0) == lax.broadcasted_iota(
        jnp.int32, (tile, tile), 1
    )
    stats = [p[rows : rows + STAT_ROWS, :tile].astype(F32) for p in parts]
    for t in range(rows // tile):
        rs = slice(t * tile, (t + 1) * tile)
        for h in range(heads):
            hs = slice(h * hd, (h + 1) * hd)
            row_at = (t * heads + h) * 3
            lses = []
            for s in stats:
                row = s[row_at : row_at + 1] + s[row_at + 1 : row_at + 2] + s[row_at + 2 : row_at + 3]
                lses.append(jnp.sum(jnp.where(eye, row, 0.0), axis=1, keepdims=True))
            peak = functools.reduce(jnp.maximum, lses)
            shares = [jnp.exp2(v - peak) for v in lses]
            total = functools.reduce(jnp.add, shares)
            mixed = functools.reduce(
                jnp.add, [s * p[rs, hs].astype(F32) for s, p in zip(shares, parts)]
            )
            whole[rs, hs] = (mixed / total).astype(BF)
    size = rows // (Z_SIZE * ys)
    for k in range(Z_SIZE):
        z_to = ring_place((ring_place(at[2]) + k) % Z_SIZE)
        for b in range(ys):
            first = pl.multiple_of((z_to * ys + (at[3] ^ b)) * size, size)
            outs[k][b * size : (b + 1) * size, :] = whole[pl.ds(first, size), :]


def merge(parts, at, rows, hd, ys):
    width = parts[0].shape[1]
    out = jax.ShapeDtypeStruct((rows // Z_SIZE, width), BF)
    return pl.pallas_call(
        functools.partial(merge_kernel, hd, len(parts), ys),
        in_specs=[pl.BlockSpec(memory_space=pltpu.SMEM)]
        + vmem(len(parts)),
        out_specs=tuple(vmem(Z_SIZE)),
        out_shape=(out,) * Z_SIZE,
        scratch_shapes=[pltpu.VMEM((rows, width), BF)],
        compiler_params=params(24),
        cost_estimate=FREE,
        name="merge",
    )(at, *parts)


def project_kernel(at, *refs):
    n = Z_SIZE
    atts, own_w = refs[:n], refs[n]
    same = refs[n + 1 : 2 * n]
    other = refs[2 * n : 3 * n - 1]
    outs = refs[3 * n - 1 :]
    half = own_w.shape[0] // 2
    total = jnp.dot(atts[0][...], own_w[...], preferred_element_type=F32)
    is_first = at[1] == 0
    for k in range(1, n):
        a = atts[k][...]
        lo, hi = a[:, :half], a[:, half:]
        mine = jnp.where(is_first, lo, hi)
        theirs = jnp.where(is_first, hi, lo)
        total += jnp.dot(mine, same[k - 1][...], preferred_element_type=F32)
        total += jnp.dot(theirs, other[k - 1][...], preferred_element_type=F32)
    size = outs[0].shape[0]
    for b, out in enumerate(outs):
        out[...] = total[b * size : (b + 1) * size].astype(BF)


def project(at, atts, own_w, same, other, count):
    rows, width = atts[0].shape[0], own_w.shape[1]
    out = jax.ShapeDtypeStruct((rows // count, width), BF)
    operands = list(atts) + [own_w] + list(same) + list(other)
    return pl.pallas_call(
        project_kernel,
        in_specs=[pl.BlockSpec(memory_space=pltpu.SMEM)]
        + vmem(len(operands)),
        out_specs=tuple(vmem(count)),
        out_shape=(out,) * count,
        compiler_params=params(24),
        cost_estimate=FREE,
        name="project",
    )(at, *operands)


def norm_kernel(x_ref, gain_ref, tail_ref, *refs):
    sums, (res_ref, a_ref, b_ref) = refs[:-3], refs[-3:]
    res = x_ref[...].astype(F32)
    res = res + functools.reduce(jnp.add, [s[...].astype(F32) for s in sums])
    res_ref[...] = res
    scale = lax.rsqrt(jnp.mean(res * res, axis=1, keepdims=True) + 1e-06)
    normed = (res * scale * gain_ref[...]).astype(BF)
    half = normed.shape[1] // 2
    a_ref[:, :half] = normed[:, :half]
    a_ref[:, half:] = tail_ref[...]
    b_ref[...] = normed[:, half:]


def norm(x, gain, tail, sums):
    rows, width = x.shape
    right = jax.ShapeDtypeStruct((rows, width // 2), BF)
    left = jax.ShapeDtypeStruct((rows, width // 2 + TAIL), BF)
    return pl.pallas_call(
        norm_kernel,
        in_specs=vmem(3 + len(sums)),
        out_specs=tuple(vmem(3)),
        out_shape=(jax.ShapeDtypeStruct((rows, width), F32), left, right),
        compiler_params=params(24),
        cost_estimate=FREE,
        name="norm",
    )(x, gain.reshape(1, width), tail, *sums)


def expert_kernel(dims, at, *refs):
    blocks, xs, ys, n_f, top, capacity = dims
    n_in, n_out = 2 * blocks * xs * ys, blocks * (xs + ys)
    ins, hbm = refs[:n_in], refs[n_in : n_in + 6]
    outs = refs[n_in + 6 : n_in + 6 + n_out]
    rows_x, acc, prod, gate_v, up_v, down_v, sems = refs[n_in + 6 + n_out :]
    tok, half = ins[-1].shape
    group = xs * ys * tok
    slots = xs * ys * capacity
    both = 2 * slots
    slabs, _, f_tile = gate_v.shape

    copies = []
    for n in range(2 * n_f):
        e, f, slab = n // n_f, n % n_f, n % slabs
        fs = pl.ds(f * f_tile, f_tile)
        copies.append(
            (
                pltpu.make_async_copy(hbm[3 * e].at[0, :, fs], gate_v.at[slab], sems.at[slab, 0]),
                pltpu.make_async_copy(hbm[3 * e + 1].at[0, :, fs], up_v.at[slab], sems.at[slab, 1]),
                pltpu.make_async_copy(hbm[3 * e + 2].at[0, fs, :], down_v.at[slab], sems.at[slab, 2]),
            )
        )
    for three in copies[:slabs]:
        for c in three:
            c.start()

    row = lax.broadcasted_iota(jnp.int32, (group, group), 0)
    col = lax.broadcasted_iota(jnp.int32, (group, group), 1)
    before = jnp.where((col < row) & (col // tok == row // tok), 1.0, 0.0).astype(BF)
    source = lax.broadcasted_iota(jnp.int32, (group, 1), 0) // tok
    lane = lax.broadcasted_iota(jnp.int32, (group, TAIL), 1)
    slot = lax.broadcasted_iota(jnp.int32, (group, both), 1)
    core_at = at[1]

    def placed(tails):
        names = tails.astype(F32)
        keys, shares = [], []
        for e in range(2):
            expert = (at[0] * 2 + (core_at ^ e)) * (Z_SIZE * ys) + at[2] * ys + at[3]
            hit = (names == expert.astype(F32)) & (lane < top)
            hits = jnp.where(hit, 1.0, 0.0)
            chosen = jnp.sum(hits, axis=1, keepdims=True)
            weight = jnp.sum(
                jnp.where(pltpu.roll(hits, top, 1) > 0.0, names, 0.0), axis=1, keepdims=True
            )
            rank = jnp.dot(
                before, jnp.broadcast_to(chosen, (group, TAIL)).astype(BF),
                preferred_element_type=F32,
            )[:, :1].astype(jnp.int32)
            keys.append(jnp.where(chosen > 0.0, e * slots + source * capacity + rank, -1))
            shares.append(weight)
        spot = (slot == keys[0]) | (slot == keys[1])
        share = jnp.where(slot < slots, shares[0], shares[1])
        return jnp.where(spot, 1.0, 0.0), jnp.where(spot, share, 0.0).astype(BF)

    puts = []
    for k in range(blocks):
        mine = ins[2 * k * xs * ys : 2 * (k + 1) * xs * ys]
        spot, put = placed(jnp.concatenate([r[:, half:] for r in mine[: xs * ys]], axis=0))
        puts.append(put)
        pick = spot.T.astype(BF)
        left = jnp.concatenate([r[:, :half] for r in mine[: xs * ys]], axis=0)
        right = jnp.concatenate([r[...] for r in mine[xs * ys :]], axis=0)
        for c, tokens in enumerate((left, right)):
            got = jnp.dot(pick, tokens, preferred_element_type=F32).astype(BF)
            for e in range(2):
                rows_x[e, k * slots : (k + 1) * slots, c * half : (c + 1) * half] = got[
                    e * slots : (e + 1) * slots
                ]

    for e in range(2):
        for f in range(n_f):
            n = e * n_f + f
            slab = n % slabs
            for c in copies[n]:
                c.wait()
            x = rows_x[e]
            gate = jnp.dot(x, gate_v[slab], preferred_element_type=F32)
            up = jnp.dot(x, up_v[slab], preferred_element_type=F32)
            hidden = (gate / (1.0 + jnp.exp(-gate)) * up).astype(BF)
            part = jnp.dot(hidden, down_v[slab], preferred_element_type=F32)
            if n + slabs < 2 * n_f:
                for c in copies[n + slabs]:
                    c.start()
            if f > 0:
                part = acc[...] + part
            if f < n_f - 1:
                acc[...] = part
            else:
                for k in range(blocks):
                    prod[k, e * slots : (e + 1) * slots, :] = part[
                        k * slots : (k + 1) * slots
                    ].astype(BF)

    for k in range(blocks):
        mine = outs[k * (xs + ys) : (k + 1) * (xs + ys)]
        put = puts[k]
        for c in range(2):
            got = jnp.dot(
                put, prod[k, :, c * half : (c + 1) * half], preferred_element_type=F32
            ).astype(BF)
            for y in range(ys):
                for x in range(xs):
                    row = (y * xs + x) * tok
                    piece = got[row : row + tok]
                    if c == 0:
                        mine[y][x] = piece
                    else:
                        mine[ys + x][y] = piece


def experts(dims, at, arrays, own, other):
    blocks, xs, ys, top, capacity = dims
    width, ffe = own[0].shape[1:]
    f_tile = 256 if ffe % 256 == 0 else ffe
    n_f = ffe // f_tile
    slots = xs * ys * capacity
    rows = blocks * slots
    any_space = [pl.BlockSpec(memory_space=pl.ANY)] * 6
    slabs = min(3, 2 * n_f)
    half = arrays[-1].shape[1]
    outs = [jax.ShapeDtypeStruct((xs, arrays[0].shape[0], half), BF)] * ys
    outs += [jax.ShapeDtypeStruct((ys, arrays[0].shape[0], half), BF)] * xs
    outs = outs * blocks
    return pl.pallas_call(
        functools.partial(expert_kernel, (blocks, xs, ys, n_f, top, capacity)),
        in_specs=[pl.BlockSpec(memory_space=pltpu.SMEM)] + vmem(len(arrays)) + any_space,
        out_specs=tuple(vmem(len(outs))),
        out_shape=tuple(outs),
        scratch_shapes=[
            pltpu.VMEM((2, rows, width), BF),
            pltpu.VMEM((rows, width), F32),
            pltpu.VMEM((blocks, 2 * slots, width), BF),
            pltpu.VMEM((slabs, width, f_tile), BF),
            pltpu.VMEM((slabs, width, f_tile), BF),
            pltpu.VMEM((slabs, f_tile, width), BF),
            pltpu.SemaphoreType.DMA((slabs, 3)),
        ],
        compiler_params=params(52),
        cost_estimate=FREE,
        name="experts",
    )(at, *arrays, *own, *other)


def add_up(*parts):
    return functools.reduce(jnp.add, [p.astype(F32) for p in parts])


def per_device(
    query_heads,
    stretch_pairs,
    cache_pairs,
    import_lists,
    file_lengths,
    layer_input,
    out_weight,
    norm_gain,
    gate_weight,
    up_weight,
    down_weight,
    expert_ids,
    route_weights,
):
    xs, ys = lax.axis_size("x"), lax.axis_size("y")
    seq_count, exp_count = xs * 2, Z_SIZE * ys
    x_at, core, z_at, y_at = (lax.axis_index(a) for a in ("x", "core", "z", "y"))
    q_rows, q_width = query_heads.shape
    _, kv_count, _, hd = stretch_pairs.shape
    local_heads = q_width // hd
    group_size = local_heads * exp_count // kv_count
    at = jnp.stack([x_at, core, z_at, y_at]).astype(jnp.int32)

    hops = range(1, seq_count)
    all_queries = [query_heads] + [
        exchange(query_heads, ("x", "core"), seq_count, hop) for hop in hops
    ]

    weights = (gate_weight, up_weight, down_weight)
    other_weights = [exchange(gate_weight, "core", 2, 1)]
    half_rows = out_weight.shape[0] // 2
    half_w = lax.dynamic_slice_in_dim(out_weight, core * half_rows, half_rows, 0)
    same_w = [ring_hop(half_w, 1)]

    block_count = cache_pairs.shape[2] // BLOCK
    cache = cache_pairs.reshape(2, kv_count, block_count, BLOCK, hd)
    score_scale = math.log2(math.e) / math.sqrt(hd)
    kv_of = lambda at: (at[2] * ys + at[3]) * local_heads // group_size
    def part(hop, queries):
        return attend(
            hop, at, import_lists, file_lengths, queries, cache, stretch_pairs, score_scale, kv_of
        )

    all_queries[-1] = later(all_queries[-1], other_weights[0])
    results = [part(hop, queries) for hop, queries in enumerate(all_queries)]
    same_w.append(ring_hop(later(same_w[-1], results[-1]), 1))
    results = results[:1] + [
        exchange(results[hop], ("x", "core"), seq_count, hop) for hop in range(1, seq_count)
    ]
    results[0] = later(results[0], same_w[1])
    pieces = merge(results, at, q_rows, hd, ys)
    same_w.append(ring_hop(same_w[-1], 1))
    pieces = later(list(pieces), same_w[2])
    other_weights.append(exchange(later(up_weight, pieces[0]), "core", 2, 1))

    attended = [pieces[0]] + [ring_hop(pieces[k], k) for k in range(1, Z_SIZE)]

    attended[0] = later(attended[0], other_weights[1])
    other_w = [exchange(p, "core", 2, 1) for p in same_w]
    shares = project(at, attended, out_weight, same_w, other_w, ys)
    other_weights.append(exchange(later(down_weight, shares[0]), "core", 2, 1))
    sums = [later(shares[0], other_weights[2])]
    sums += [exchange(shares[b], "y", ys, b) for b in range(1, ys)]
    tail = jnp.concatenate([expert_ids.astype(BF), route_weights.astype(BF)], axis=1)
    tail = jnp.pad(tail, ((0, 0), (0, TAIL - tail.shape[1])))
    residual, left, right = norm(layer_input, norm_gain, tail, sums)

    gathered = []
    for k in range(Z_SIZE):
        firsts = [left] + [exchange(left, "x", xs, r) for r in range(1, xs)]
        seconds = [right] + [exchange(right, "y", ys, r) for r in range(1, ys)]
        after_left, after_right = left, right
        if k + 1 < Z_SIZE:
            after_left, after_right = ring_hop(left, 1), ring_hop(right, 1)
        gathered += firsts
        gathered += [exchange(f, "y", ys, r) for r in range(1, ys) for f in firsts]
        by_x = [seconds] + [[exchange(f, "x", xs, r) for f in seconds] for r in range(1, xs)]
        gathered += [by_x[x][y] for y in range(ys) for x in range(xs)]
        left, right = after_left, after_right

    token_count, top_k = expert_ids.shape
    expert_total = seq_count * exp_count
    capacity = min(token_count, max(2, token_count * top_k * 5 // (4 * expert_total)))
    partial = experts(
        (Z_SIZE, xs, ys, top_k, capacity), at, gathered, weights, other_weights
    )

    lines = {"x": [], "y": []}

    def send(value, axis, size, hop, lag=LAG):
        line = lines[axis]
        if lag and len(line) >= lag:
            value, _ = lax.optimization_barrier((value, line[-lag]))
        line.append(exchange(value, axis, size, hop))
        return line[-1]

    total = None
    for k in [*range(1, Z_SIZE), 0]:
        mine = partial[k * (xs + ys) : (k + 1) * (xs + ys)]
        halves = []
        for piles, (far, n_far), (near, n_near) in (
            (mine[:ys], ("y", ys), ("x", xs)),
            (mine[ys:], ("x", xs), ("y", ys)),
        ):
            got = [send(piles[r], far, n_far, r) for r in range(1, n_far)]
            halves.append((add_up(piles[0], *got), near, n_near))
        halves = [
            add_up(h[0], *[send(h[r].astype(BF), near, n, r) for r in range(1, n)])
            for h, near, n in halves
        ]
        if total is not None:
            halves = [add_up(h, t) for h, t in zip(halves, ring_hop(total, 1))]
        total = jnp.stack(halves).astype(BF) if k else halves
    return (residual + jnp.concatenate(total, axis=1)).astype(BF)


def solution(mesh):
    seq, exp = mesh.shape["seq"], mesh.shape["exp"]
    fine = Mesh(
        mesh.devices.reshape(seq // 2, 2, Z_SIZE, exp // Z_SIZE), ("x", "core", "z", "y")
    )
    s, e = ("x", "core"), ("z", "y")
    both = s + e
    in_specs = (
        P(s, e),
        P(None, None, s, None),
        P(None, None, s, None),
        P(),
        P(),
        P(both, None),
        P(e, None),
        P(),
        P(both, None, None),
        P(both, None, None),
        P(both, None, None),
        P(both, None),
        P(both, None),
    )
    return jax.shard_map(
        per_device, mesh=fine, in_specs=in_specs, out_specs=P(both, None), check_vma=False
    )
```

```python
import functools
import math

import jax
import jax.numpy as jnp
from jax import lax
from jax.experimental import pallas as pl
from jax.experimental.pallas import tpu as pltpu
from jax.sharding import Mesh
from jax.sharding import PartitionSpec as P

BLOCK = 512
CAP_B = 2
Z_SIZE = 4
RING = (0, 1, 3, 2)
NEG_FLOOR = -1e30
BF = jnp.bfloat16
F32 = jnp.float32
MIB = 1 << 20
STAT_ROWS = 16
TAIL = 128
ATT = 10
LAG = 3
FREE = pl.CostEstimate(flops=0, bytes_accessed=0, transcendentals=0)


def vmem(count):
    return [pl.BlockSpec(memory_space=pltpu.VMEM)] * count


def params(mib):
    return pltpu.CompilerParams(vmem_limit_bytes=mib * MIB)


def exchange(value, axis, size, hop):
    return lax.ppermute(value, axis, [(i, i ^ hop) for i in range(size)])


def later(value, than):
    return lax.optimization_barrier((value, than))[0]


def ring_hop(value, hops):
    n = len(RING)
    return lax.ppermute(value, "z", [(RING[i], RING[(i + hops) % n]) for i in range(n)])


def listed_block(hop, per_index, slot, at, lists, lens):
    seq_index = at[0] * 2 + at[1]
    shard = seq_index ^ hop
    found, block, present = jnp.int32(0), jnp.int32(0), jnp.int32(0)
    for n in range(lists.shape[1]):
        named = lists[shard, n]
        here = named // per_index == seq_index
        hit = here & (found == slot)
        block = jnp.where(hit, named % per_index, block)
        present = jnp.where(hit, 1, present)
        found = found + here.astype(jnp.int32)
    return block, present


def attend_kernel(scale, hop, per_index, at, lists, lens, q_ref, kb0, kb1, vb0, vb1, ks, vs, out_ref):
    rows, width = q_ref.shape
    hd = kb0.shape[-1]
    heads = width // hd
    tile = min(256, rows, width)
    tiles = rows // tile
    eye = lax.broadcasted_iota(jnp.int32, (tile, tile), 0) == lax.broadcasted_iota(
        jnp.int32, (tile, tile), 1
    )
    valid = [listed_block(hop, per_index, n, at, lists, lens)[1] > 0 for n in range(CAP_B)]
    always = lists.shape[1] == CAP_B * lists.shape[0]
    seq_index = at[0] * 2 + at[1]
    q_first, k_first = (seq_index ^ hop) * rows, seq_index * rows
    nt = (((1,), (1,)), ((), ()))

    def first_of_file(pos):
        offset, start = jnp.int32(0), jnp.zeros_like(pos)
        for n in range(lens.shape[0]):
            start = jnp.where(offset <= pos, offset, start)
            offset = offset + lens[n]
        return start

    needed = (k_first <= q_first + rows - 1) & (
        k_first + ks.shape[-2] - 1 >= first_of_file(q_first)
    )

    def run(with_local):
        stat_row = lax.broadcasted_iota(jnp.int32, (STAT_ROWS, tile), 0)

        def step(n, stat):
            t, h = n // heads, n % heads
            rs = pl.ds(pl.multiple_of(t * tile, tile), tile)
            hs = pl.ds(pl.multiple_of(h * hd, hd), hd)
            q = q_ref[rs, hs]

            def scores(k_ref):
                k = k_ref[...].reshape(k_ref.shape[-2], hd)
                return lax.dot_general(q, k, nt, preferred_element_type=F32) * scale

            parts = [scores(kb0), scores(kb1)]
            if not always:
                parts = [jnp.where(v, p, NEG_FLOOR) for v, p in zip(valid, parts)]
            values = [vb0, vb1]
            if with_local:
                kpos = k_first + lax.broadcasted_iota(jnp.int32, (tile, ks.shape[-2]), 1)
                qpos = q_first + t * tile + lax.broadcasted_iota(jnp.int32, (tile, 1), 0)
                allowed = (kpos <= qpos) & (kpos >= first_of_file(qpos))
                parts.append(jnp.where(allowed, scores(ks), NEG_FLOOR))
                values.append(vs)
            peak = functools.reduce(
                jnp.maximum, [jnp.max(p, axis=1, keepdims=True) for p in parts]
            )
            total = jnp.zeros((tile, 1), F32)
            numer = jnp.zeros((tile, hd), F32)
            for p, v_ref in zip(parts, values):
                w = jnp.exp2(p - peak)
                total = total + jnp.sum(w, axis=1, keepdims=True)
                v = v_ref[...].reshape(v_ref.shape[-2], hd)
                numer = numer + jnp.dot(w.astype(BF), v, preferred_element_type=F32)
            out_ref[rs, hs] = (numer / total).astype(BF)
            lse = peak + jnp.log2(total)
            row = jnp.sum(jnp.where(eye, lse, 0.0), axis=0, keepdims=True)
            high = row.astype(BF).astype(F32)
            mid = (row - high).astype(BF).astype(F32)
            low = row - high - mid
            for i, piece in enumerate((high, mid, low)):
                stat = jnp.where(stat_row == 3 * n + i, piece, stat)
            return stat

        stat = lax.fori_loop(0, tiles * heads, step, jnp.zeros((STAT_ROWS, tile), F32))
        out_ref[rows : rows + STAT_ROWS, :] = jnp.concatenate(
            [stat] * (width // tile), axis=1
        ).astype(BF)

    @pl.when(needed)
    def _():
        run(True)

    @pl.when(jnp.logical_not(needed))
    def _():
        run(False)


def attend(hop, at, lists, lens, queries, cache, stretch, scale, kv_of):
    rows, width = queries.shape
    per_index, hd = cache.shape[2], cache.shape[-1]

    def cache_spec(which, slot):
        def index(i, *sc):
            return which, kv_of(sc[0]), listed_block(hop, per_index, slot, *sc)[0], 0, 0

        return pl.BlockSpec((1, 1, 1, BLOCK, hd), index)

    def stretch_spec(which):
        return pl.BlockSpec(
            (1, 1) + stretch.shape[2:], lambda i, *sc: (which, kv_of(sc[0]), 0, 0)
        )

    whole = lambda shape: pl.BlockSpec(shape, lambda i, *sc: (0,) * len(shape))
    return pl.pallas_call(
        functools.partial(attend_kernel, scale, hop, per_index),
        grid_spec=pltpu.PrefetchScalarGridSpec(
            num_scalar_prefetch=3,
            grid=(1,),
            in_specs=[
                whole(queries.shape),
                cache_spec(0, 0),
                cache_spec(0, 1),
                cache_spec(1, 0),
                cache_spec(1, 1),
                stretch_spec(0),
                stretch_spec(1),
            ],
            out_specs=whole((rows + STAT_ROWS, width)),
        ),
        out_shape=jax.ShapeDtypeStruct((rows + STAT_ROWS, width), BF),
        compiler_params=params(56),
        cost_estimate=pl.CostEstimate(
            flops=ATT * 4 * rows * width * 3 * BLOCK,
            bytes_accessed=2 * MIB,
            transcendentals=rows * width // hd * 3 * BLOCK,
        ),
        name="attend",
    )(at, lists, lens, queries, cache, cache, cache, cache, stretch, stretch)


def ring_place(z):
    return jnp.where(z < 2, z, 5 - z)


def merge_kernel(hd, n_parts, ys, at, *refs):
    parts, outs = refs[:n_parts], refs[n_parts : n_parts + Z_SIZE]
    whole = refs[-1]
    rows, width = whole.shape
    heads = width // hd
    tile = min(256, rows, width)
    eye = lax.broadcasted_iota(jnp.int32, (tile, tile), 0) == lax.broadcasted_iota(
        jnp.int32, (tile, tile), 1
    )
    stats = [p[rows : rows + STAT_ROWS, :tile].astype(F32) for p in parts]
    for t in range(rows // tile):
        rs = slice(t * tile, (t + 1) * tile)
        for h in range(heads):
            hs = slice(h * hd, (h + 1) * hd)
            row_at = (t * heads + h) * 3
            lses = []
            for s in stats:
                row = s[row_at : row_at + 1] + s[row_at + 1 : row_at + 2] + s[row_at + 2 : row_at + 3]
                lses.append(jnp.sum(jnp.where(eye, row, 0.0), axis=1, keepdims=True))
            peak = functools.reduce(jnp.maximum, lses)
            shares = [jnp.exp2(v - peak) for v in lses]
            total = functools.reduce(jnp.add, shares)
            mixed = functools.reduce(
                jnp.add, [s * p[rs, hs].astype(F32) for s, p in zip(shares, parts)]
            )
            whole[rs, hs] = (mixed / total).astype(BF)
    size = rows // (Z_SIZE * ys)
    for k in range(Z_SIZE):
        z_to = ring_place((ring_place(at[2]) + k) % Z_SIZE)
        for b in range(ys):
            first = pl.multiple_of((z_to * ys + (at[3] ^ b)) * size, size)
            outs[k][b * size : (b + 1) * size, :] = whole[pl.ds(first, size), :]


def merge(parts, at, rows, hd, ys):
    width = parts[0].shape[1]
    out = jax.ShapeDtypeStruct((rows // Z_SIZE, width), BF)
    return pl.pallas_call(
        functools.partial(merge_kernel, hd, len(parts), ys),
        in_specs=[pl.BlockSpec(memory_space=pltpu.SMEM)]
        + vmem(len(parts)),
        out_specs=tuple(vmem(Z_SIZE)),
        out_shape=(out,) * Z_SIZE,
        scratch_shapes=[pltpu.VMEM((rows, width), BF)],
        compiler_params=params(24),
        cost_estimate=FREE,
        name="merge",
    )(at, *parts)


def project_kernel(at, *refs):
    n = Z_SIZE
    atts, own_w = refs[:n], refs[n]
    same = refs[n + 1 : 2 * n]
    other, outs = refs[2 * n], refs[2 * n + 1 :]
    half = own_w.shape[0] // 2
    total = jnp.dot(atts[0][...], own_w[...], preferred_element_type=F32)
    is_first = at[1] == 0
    for k in range(1, n):
        a = atts[k][...]
        lo, hi = a[:, :half], a[:, half:]
        mine = jnp.where(is_first, lo, hi)
        theirs = jnp.where(is_first, hi, lo)
        total += jnp.dot(mine, same[k - 1][...], preferred_element_type=F32)
        total += jnp.dot(theirs, other[k - 1], preferred_element_type=F32)
    size = outs[0].shape[0]
    for b, out in enumerate(outs):
        out[...] = total[b * size : (b + 1) * size].astype(BF)


def project(at, atts, own_w, same, other, count):
    rows, width = atts[0].shape[0], own_w.shape[1]
    out = jax.ShapeDtypeStruct((rows // count, width), BF)
    operands = list(atts) + [own_w] + list(same) + [other]
    return pl.pallas_call(
        project_kernel,
        in_specs=[pl.BlockSpec(memory_space=pltpu.SMEM)]
        + vmem(len(operands)),
        out_specs=tuple(vmem(count)),
        out_shape=(out,) * count,
        compiler_params=params(24),
        cost_estimate=FREE,
        name="project",
    )(at, *operands)


def norm_kernel(x_ref, gain_ref, tail_ref, *refs):
    sums, (res_ref, a_ref, b_ref) = refs[:-3], refs[-3:]
    res = x_ref[...].astype(F32)
    res = res + functools.reduce(jnp.add, [s[...].astype(F32) for s in sums])
    res_ref[...] = res
    scale = lax.rsqrt(jnp.mean(res * res, axis=1, keepdims=True) + 1e-06)
    normed = (res * scale * gain_ref[...]).astype(BF)
    half = normed.shape[1] // 2
    a_ref[:, :half] = normed[:, :half]
    a_ref[:, half:] = tail_ref[...]
    b_ref[...] = normed[:, half:]


def norm(x, gain, tail, sums):
    rows, width = x.shape
    right = jax.ShapeDtypeStruct((rows, width // 2), BF)
    left = jax.ShapeDtypeStruct((rows, width // 2 + TAIL), BF)
    return pl.pallas_call(
        norm_kernel,
        in_specs=vmem(3 + len(sums)),
        out_specs=tuple(vmem(3)),
        out_shape=(jax.ShapeDtypeStruct((rows, width), F32), left, right),
        compiler_params=params(24),
        cost_estimate=FREE,
        name="norm",
    )(x, gain.reshape(1, width), tail, *sums)


def expert_kernel(dims, at, *refs):
    blocks, xs, ys, n_f, top, capacity = dims
    n_in, n_out = 2 * blocks * xs * ys, blocks * (xs + ys)
    ins, hbm = refs[:n_in], refs[n_in : n_in + 6]
    outs = refs[n_in + 6 : n_in + 6 + n_out]
    rows_x, acc, prod, gate_v, up_v, down_v, sems = refs[n_in + 6 + n_out :]
    tok, half = ins[-1].shape
    group = xs * ys * tok
    slots = xs * ys * capacity
    both = 2 * slots
    slabs, _, f_tile = gate_v.shape

    copies = []
    for n in range(2 * n_f):
        e, f, slab = n // n_f, n % n_f, n % slabs
        fs = pl.ds(f * f_tile, f_tile)
        copies.append(
            (
                pltpu.make_async_copy(hbm[3 * e].at[0, :, fs], gate_v.at[slab], sems.at[slab, 0]),
                pltpu.make_async_copy(hbm[3 * e + 1].at[0, :, fs], up_v.at[slab], sems.at[slab, 1]),
                pltpu.make_async_copy(hbm[3 * e + 2].at[0, fs, :], down_v.at[slab], sems.at[slab, 2]),
            )
        )
    for three in copies[:slabs]:
        for c in three:
            c.start()

    row = lax.broadcasted_iota(jnp.int32, (group, group), 0)
    col = lax.broadcasted_iota(jnp.int32, (group, group), 1)
    before = jnp.where((col < row) & (col // tok == row // tok), 1.0, 0.0).astype(BF)
    source = lax.broadcasted_iota(jnp.int32, (group, 1), 0) // tok
    lane = lax.broadcasted_iota(jnp.int32, (group, TAIL), 1)
    slot = lax.broadcasted_iota(jnp.int32, (group, both), 1)
    core_at = at[1]

    def placed(tails):
        names = tails.astype(F32)
        keys, shares = [], []
        for e in range(2):
            expert = (at[0] * 2 + (core_at ^ e)) * (Z_SIZE * ys) + at[2] * ys + at[3]
            hit = (names == expert.astype(F32)) & (lane < top)
            hits = jnp.where(hit, 1.0, 0.0)
            chosen = jnp.sum(hits, axis=1, keepdims=True)
            weight = jnp.sum(
                jnp.where(pltpu.roll(hits, top, 1) > 0.0, names, 0.0), axis=1, keepdims=True
            )
            rank = jnp.dot(
                before, jnp.broadcast_to(chosen, (group, TAIL)).astype(BF),
                preferred_element_type=F32,
            )[:, :1].astype(jnp.int32)
            keys.append(jnp.where(chosen > 0.0, e * slots + source * capacity + rank, -1))
            shares.append(weight)
        spot = (slot == keys[0]) | (slot == keys[1])
        share = jnp.where(slot < slots, shares[0], shares[1])
        return jnp.where(spot, 1.0, 0.0), jnp.where(spot, share, 0.0).astype(BF)

    puts = []
    for k in range(blocks):
        mine = ins[2 * k * xs * ys : 2 * (k + 1) * xs * ys]
        spot, put = placed(jnp.concatenate([r[:, half:] for r in mine[: xs * ys]], axis=0))
        puts.append(put)
        pick = spot.T.astype(BF)
        left = jnp.concatenate([r[:, :half] for r in mine[: xs * ys]], axis=0)
        right = jnp.concatenate([r[...] for r in mine[xs * ys :]], axis=0)
        for c, tokens in enumerate((left, right)):
            got = jnp.dot(pick, tokens, preferred_element_type=F32).astype(BF)
            for e in range(2):
                rows_x[e, k * slots : (k + 1) * slots, c * half : (c + 1) * half] = got[
                    e * slots : (e + 1) * slots
                ]

    for e in range(2):
        for f in range(n_f):
            n = e * n_f + f
            slab = n % slabs
            for c in copies[n]:
                c.wait()
            x = rows_x[e]
            gate = jnp.dot(x, gate_v[slab], preferred_element_type=F32)
            up = jnp.dot(x, up_v[slab], preferred_element_type=F32)
            hidden = (gate / (1.0 + jnp.exp(-gate)) * up).astype(BF)
            part = jnp.dot(hidden, down_v[slab], preferred_element_type=F32)
            if n + slabs < 2 * n_f:
                for c in copies[n + slabs]:
                    c.start()
            if f > 0:
                part = acc[...] + part
            if f < n_f - 1:
                acc[...] = part
            else:
                for k in range(blocks):
                    prod[k, e * slots : (e + 1) * slots, :] = part[
                        k * slots : (k + 1) * slots
                    ].astype(BF)

    for k in range(blocks):
        mine = outs[k * (xs + ys) : (k + 1) * (xs + ys)]
        put = puts[k]
        for c in range(2):
            got = jnp.dot(
                put, prod[k, :, c * half : (c + 1) * half], preferred_element_type=F32
            ).astype(BF)
            for y in range(ys):
                for x in range(xs):
                    row = (y * xs + x) * tok
                    piece = got[row : row + tok]
                    if c == 0:
                        mine[y][x] = piece
                    else:
                        mine[ys + x][y] = piece


def experts(dims, at, arrays, own, other):
    blocks, xs, ys, top, capacity = dims
    width, ffe = own[0].shape[1:]
    f_tile = 256 if ffe % 256 == 0 else ffe
    n_f = ffe // f_tile
    slots = xs * ys * capacity
    rows = blocks * slots
    any_space = [pl.BlockSpec(memory_space=pl.ANY)] * 6
    slabs = min(3, 2 * n_f)
    half = arrays[-1].shape[1]
    outs = [jax.ShapeDtypeStruct((xs, arrays[0].shape[0], half), BF)] * ys
    outs += [jax.ShapeDtypeStruct((ys, arrays[0].shape[0], half), BF)] * xs
    outs = outs * blocks
    return pl.pallas_call(
        functools.partial(expert_kernel, (blocks, xs, ys, n_f, top, capacity)),
        in_specs=[pl.BlockSpec(memory_space=pltpu.SMEM)] + vmem(len(arrays)) + any_space,
        out_specs=tuple(vmem(len(outs))),
        out_shape=tuple(outs),
        scratch_shapes=[
            pltpu.VMEM((2, rows, width), BF),
            pltpu.VMEM((rows, width), F32),
            pltpu.VMEM((blocks, 2 * slots, width), BF),
            pltpu.VMEM((slabs, width, f_tile), BF),
            pltpu.VMEM((slabs, width, f_tile), BF),
            pltpu.VMEM((slabs, f_tile, width), BF),
            pltpu.SemaphoreType.DMA((slabs, 3)),
        ],
        compiler_params=params(52),
        cost_estimate=FREE,
        name="experts",
    )(at, *arrays, *own, *other)


def add_up(*parts):
    return functools.reduce(jnp.add, [p.astype(F32) for p in parts])


def per_device(
    query_heads,
    stretch_pairs,
    cache_pairs,
    import_lists,
    file_lengths,
    layer_input,
    out_weight,
    norm_gain,
    gate_weight,
    up_weight,
    down_weight,
    expert_ids,
    route_weights,
):
    xs, ys = lax.axis_size("x"), lax.axis_size("y")
    seq_count, exp_count = xs * 2, Z_SIZE * ys
    x_at, core, z_at, y_at = (lax.axis_index(a) for a in ("x", "core", "z", "y"))
    q_rows, q_width = query_heads.shape
    _, kv_count, _, hd = stretch_pairs.shape
    local_heads = q_width // hd
    group_size = local_heads * exp_count // kv_count
    at = jnp.stack([x_at, core, z_at, y_at]).astype(jnp.int32)

    hops = range(1, seq_count)
    all_queries = [query_heads] + [
        exchange(query_heads, ("x", "core"), seq_count, hop) for hop in hops
    ]

    weights = (gate_weight, up_weight, down_weight)
    other_weights = [exchange(gate_weight, "core", 2, 1)]
    half_rows = out_weight.shape[0] // 2
    half_w = lax.dynamic_slice_in_dim(out_weight, core * half_rows, half_rows, 0)
    same_w = [ring_hop(half_w, 1)]

    block_count = cache_pairs.shape[2] // BLOCK
    cache = cache_pairs.reshape(2, kv_count, block_count, BLOCK, hd)
    score_scale = math.log2(math.e) / math.sqrt(hd)
    kv_of = lambda at: (at[2] * ys + at[3]) * local_heads // group_size
    def part(hop, queries):
        return attend(
            hop, at, import_lists, file_lengths, queries, cache, stretch_pairs, score_scale, kv_of
        )

    all_queries[-1] = later(all_queries[-1], other_weights[0])
    results = [part(hop, queries) for hop, queries in enumerate(all_queries)]
    same_w.append(ring_hop(later(same_w[-1], results[-1]), 1))
    results = results[:1] + [
        exchange(results[hop], ("x", "core"), seq_count, hop) for hop in range(1, seq_count)
    ]
    results[0] = later(results[0], same_w[1])
    pieces = merge(results, at, q_rows, hd, ys)
    same_w.append(ring_hop(same_w[-1], 1))
    pieces = later(list(pieces), same_w[2])
    other_weights.append(exchange(later(up_weight, pieces[0]), "core", 2, 1))

    attended = [pieces[0]] + [ring_hop(pieces[k], k) for k in range(1, Z_SIZE)]

    attended[0] = later(attended[0], other_weights[1])
    other_w = exchange(jnp.stack(same_w), "core", 2, 1)
    shares = project(at, attended, out_weight, same_w, other_w, ys)
    other_weights.append(exchange(later(down_weight, shares[0]), "core", 2, 1))
    sums = [later(shares[0], other_weights[2])]
    sums += [exchange(shares[b], "y", ys, b) for b in range(1, ys)]
    tail = jnp.concatenate([expert_ids.astype(BF), route_weights.astype(BF)], axis=1)
    tail = jnp.pad(tail, ((0, 0), (0, TAIL - tail.shape[1])))
    residual, left, right = norm(layer_input, norm_gain, tail, sums)

    gathered = []
    for k in range(Z_SIZE):
        firsts = [left] + [exchange(left, "x", xs, r) for r in range(1, xs)]
        seconds = [right] + [exchange(right, "y", ys, r) for r in range(1, ys)]
        after_left, after_right = left, right
        if k + 1 < Z_SIZE:
            after_left, after_right = ring_hop(left, 1), ring_hop(right, 1)
        gathered += firsts
        gathered += [exchange(f, "y", ys, r) for r in range(1, ys) for f in firsts]
        by_x = [seconds] + [[exchange(f, "x", xs, r) for f in seconds] for r in range(1, xs)]
        gathered += [by_x[x][y] for y in range(ys) for x in range(xs)]
        left, right = after_left, after_right

    token_count, top_k = expert_ids.shape
    expert_total = seq_count * exp_count
    capacity = min(token_count, max(2, token_count * top_k * 5 // (4 * expert_total)))
    partial = experts(
        (Z_SIZE, xs, ys, top_k, capacity), at, gathered, weights, other_weights
    )

    lines = {"x": [], "y": []}

    def send(value, axis, size, hop, lag=LAG):
        line = lines[axis]
        if lag and len(line) >= lag:
            value, _ = lax.optimization_barrier((value, line[-lag]))
        line.append(exchange(value, axis, size, hop))
        return line[-1]

    total = None
    for k in [*range(1, Z_SIZE), 0]:
        mine = partial[k * (xs + ys) : (k + 1) * (xs + ys)]
        halves = []
        for piles, (far, n_far), (near, n_near) in (
            (mine[:ys], ("y", ys), ("x", xs)),
            (mine[ys:], ("x", xs), ("y", ys)),
        ):
            got = [send(piles[r], far, n_far, r) for r in range(1, n_far)]
            halves.append((add_up(piles[0], *got), near, n_near))
        halves = [
            add_up(h[0], *[send(h[r].astype(BF), near, n, r) for r in range(1, n)])
            for h, near, n in halves
        ]
        if total is not None:
            halves = [add_up(h, t) for h, t in zip(halves, ring_hop(total, 1))]
        total = jnp.stack(halves).astype(BF) if k else halves
    return (residual + jnp.concatenate(total, axis=1)).astype(BF)


def solution(mesh):
    seq, exp = mesh.shape["seq"], mesh.shape["exp"]
    fine = Mesh(
        mesh.devices.reshape(seq // 2, 2, Z_SIZE, exp // Z_SIZE), ("x", "core", "z", "y")
    )
    s, e = ("x", "core"), ("z", "y")
    both = s + e
    in_specs = (
        P(s, e),
        P(None, None, s, None),
        P(None, None, s, None),
        P(),
        P(),
        P(both, None),
        P(e, None),
        P(),
        P(both, None, None),
        P(both, None, None),
        P(both, None, None),
        P(both, None),
        P(both, None),
    )
    return jax.shard_map(
        per_device, mesh=fine, in_specs=in_specs, out_specs=P(both, None), check_vma=False
    )
```
